512 devices in a mesh: tm: 4 (over z_hi, core), space: 128 (over z_lo, y, x).
Axes of the slice: x: 4, y: 4, z: 16 (z_hi: 2, z_lo: 8; z = z_hi * 8 + z_lo), core: 2. Of those that a mesh axis runs over, the one named last changes fastest.
Arguments:
- initial: float32 [256, 64, 256], P('space'), may hold values from -1 to 1
- guess: float32 [4, 256, 64, 256], P('tm', 'space'), may hold values from -1 to 1
Outputs:
- states: float32 [4, 256, 64, 256], P('tm', 'space')
The draws below stay inside these ranges and needn't reach their ends.
All inputs are finite; a program needn't handle non-finite values.
Results may differ from the reference program's by a relative error of at most 0.0001.
Values sent between devices are 32-bit elements; how exact they have to be, the bound alone decides.
A program may use at most 64 MiB of HBM per device.

```python
import jax
import jax.numpy as jnp

NY = 64
NX = 256
ITERS = 2
SLICES = 4
NZ = 256


def block_scale(rng, extent, pieces, least, largest):
    def one(dim, parts):
        heights = jax.random.uniform(jax.random.fold_in(jax.random.fold_in(rng, 6), dim), (parts,), jnp.float32, least / len(pieces), largest / len(pieces))
        return jnp.repeat(jnp.exp(heights), extent[dim] // parts).reshape((-1,) + (1,) * (len(extent) - dim - 1))

    loudness = one(*pieces[0])
    for cut in pieces[1:]:
        loudness = loudness * one(*cut)
    return loudness


def setup_inputs(seed: int = 0) -> dict:
    seeds = jax.random.split(jax.random.key(seed), 3)
    initial = jnp.clip(jax.random.uniform(seeds[0], (NZ, NY, NX), jnp.float32, -1.0, 1.0) * block_scale(seeds[0], (NZ, NY, NX), ((0, 128),), -0.4, 0.0), -1.0, 1.0)
    guess = jnp.clip(jax.random.uniform(seeds[1], (SLICES, NZ, NY, NX), jnp.float32, -1.0, 1.0) * block_scale(seeds[1], (SLICES, NZ, NY, NX), ((0, 4), (1, 128)), -0.4, 0.0), -1.0, 1.0)
    return dict(initial=initial, guess=guess)


time_step = 0.24
half_step = 0.12


def laplace(field):
    total = jnp.roll(field, 1, -3) + jnp.roll(field, -1, -3)
    total = total + jnp.roll(field, 1, -2) + jnp.roll(field, -1, -2)
    total = total + jnp.roll(field, 1, -1) + jnp.roll(field, -1, -1)
    return total - 6.0 * field


def fine_force(field):
    return laplace(field) + field - field * field * field


def coarse_force(field):
    return 0.25 * laplace(field) + field - field * field * field


def restrict(field):
    lead = field.shape[:-3]
    depth, rows, cols = field.shape[-3:]
    blocks = field.reshape(lead + (depth // 2, 2, rows // 2, 2, cols // 2, 2))
    count = len(lead)
    return jnp.mean(blocks, axis=(count + 1, count + 3, count + 5))


def prolong(field):
    field = jnp.repeat(field, 2, axis=-3)
    field = jnp.repeat(field, 2, axis=-2)
    return jnp.repeat(field, 2, axis=-1)


def advance(forces, start, force_fn):
    first_int = time_step * (5.0 / 24.0 * forces[0] + 1.0 / 3.0 * forces[1] - 1.0 / 24.0 * forces[2])
    second_int = time_step * (-1.0 / 24.0 * forces[0] + 1.0 / 3.0 * forces[1] + 5.0 / 24.0 * forces[2])
    node_zero = start
    node_one = node_zero + half_step * (force_fn(node_zero) - forces[0]) + first_int
    node_two = node_one + half_step * (force_fn(node_one) - forces[1]) + second_int
    return [node_zero, node_one, node_two]


def reference(initial, guess):
    nodes = [guess, guess, guess]
    coarse_init = restrict(initial)
    for iteration in range(ITERS):
        fine_start = jnp.concatenate([initial[None], nodes[2][:-1]], axis=0)
        restricted = [restrict(value) for value in nodes]
        results = []
        start = coarse_init
        for slice_index in range(SLICES):
            olds = [value[slice_index] for value in restricted]
            forces = [coarse_force(value) for value in olds]
            swept = advance(forces, start, coarse_force)
            results.append(swept)
            start = swept[2]
        corrected = []
        for number in range(3):
            stacked = jnp.stack([results[s][number] for s in range(SLICES)])
            corrected.append(nodes[number] + prolong(stacked - restricted[number]))
        forces = [fine_force(value) for value in corrected]
        nodes = advance(forces, fine_start, fine_force)
    return nodes[2]
```

```python
import functools

import jax
import jax.numpy as jnp
from jax import lax
from jax.experimental import pallas as pl
from jax.experimental.pallas import tpu as pltpu
from jax.sharding import PartitionSpec as P

MESH = pl.DeviceIdType.MESH
DT, H = 0.24, 0.12
A = (DT * 5.0 / 24.0 - H, DT / 3.0, -DT / 24.0)
B = (-DT / 24.0, DT / 3.0 - H, DT * 5.0 / 24.0)
REACH = 9
DEEP = 5


def split(x):
    high = x.astype(jnp.bfloat16)
    rest = x - high.astype(jnp.float32)
    mid = rest.astype(jnp.bfloat16)
    low = (rest - mid.astype(jnp.float32)).astype(jnp.bfloat16)
    return jnp.concatenate([high, mid, low], axis=0)


def permuted(x, perm):
    rows = x.shape[0]
    out = jnp.dot(split(x), perm, preferred_element_type=jnp.float32)
    return out[:rows] + (out[rows : 2 * rows] + out[2 * rows :])


def perm_matrix(to_parity):
    i = lax.broadcasted_iota(jnp.int32, (256, 256), 0)
    j = lax.broadcasted_iota(jnp.int32, (256, 256), 1)
    wide, packed = (i, j) if to_parity else (j, i)
    lane = jnp.where(packed < 128, 2 * packed, 2 * packed - 255)
    return jnp.where(wide == lane, 1.0, 0.0).astype(jnp.bfloat16)


def lane_roll(x, by):
    return pltpu.roll(x, by % 128, 1)


def row_roll(x, by):
    return pltpu.roll(x, by % 32, 0)


def coarse_sum(below, x, above):
    total = below + above
    total = total + lane_roll(x, 1) + lane_roll(x, -1)
    return total + row_roll(x, 1) + row_roll(x, -1)


def euler(below, x, above):
    return 0.25 * H * coarse_sum(below, x, above) + x * ((1.0 - 0.5 * H) - H * (x * x))


def cube(x):
    return x * x * x


def mix(weights, values):
    return weights[0] * values[0] + weights[1] * values[1] + weights[2] * values[2]


def sub(ref, plane, part):
    return ref[plane, 32 * part : 32 * part + 32, :]


def restricted(ref, first):
    total = None
    for plane in (first, first + 1):
        for part in range(4):
            piece = sub(ref, plane, part)
            total = piece if total is None else total + piece
    return 0.125 * total


def fine_sum(ref, plane, part):
    row, col = part // 2, part % 2
    beside = sub(ref, plane, row * 2 + 1 - col)
    over = sub(ref, plane, (1 - row) * 2 + col)
    total = sub(ref, plane - 1, part) + sub(ref, plane + 1, part)
    total = total + beside + lane_roll(beside, 1 if col == 0 else -1)
    return total + over + row_roll(over, 1 if row == 0 else -1)


def fine_sweep(nodes, shifts, start, z1, z2, q1, q2, d2, out1, first1, out2, first2):
    for plane in range(6):
        for part in range(4):
            rows = slice(32 * part, 32 * part + 32)
            u = [sub(nodes[m], plane, part) + shifts[m][plane // 2] for m in range(3)]
            n0 = sub(start, plane, part)
            z = H * n0 + mix(A, u)
            z1[plane, rows, :] = z
            if 1 <= plane <= 4:
                cubes = [cube(v) for v in u]
                q1[plane, rows, :] = n0 - 5.0 * z - (H * cube(n0) + mix(A, cubes))
                d2[plane, rows, :] = mix(B, u)
                if 2 <= plane <= 3:
                    q2[plane, rows, :] = mix(B, cubes)
    for plane in range(1, 5):
        for part in range(4):
            rows = slice(32 * part, 32 * part + 32)
            n1 = sub(q1, plane, part) + fine_sum(z1, plane, part)
            z = H * n1 + sub(d2, plane, part)
            z2[plane, rows, :] = z
            if 2 <= plane <= 3:
                if out1 is not None:
                    out1[first1 + plane - 2, rows, :] = n1
                q2[plane, rows, :] = n1 - 5.0 * z - (H * cube(n1) + sub(q2, plane, part))
    for plane in range(2, 4):
        for part in range(4):
            rows = slice(32 * part, 32 * part + 32)
            out2[first2 + plane - 2, rows, :] = sub(q2, plane, part) + fine_sum(z2, plane, part)


def kernel(
    ns, nt,
    init_ref, guess_ref, out_ref,
    g, f, n1, n2, f2,
    z1, z2, q1, q2, d2,
    ic, sa, sb, w, v, c1, c2, s, t1, t2, halves,
    ssem, rsem,
):
    t = lax.axis_index("tm")
    c = lax.axis_index("space")
    even = lax.rem(t, 2) == 0

    def at(by):
        return (t, lax.rem(c + by + ns, ns))

    up = (jnp.minimum(t + 1, nt - 1), c)
    down = (jnp.maximum(t - 1, 0), c)

    barrier = pltpu.get_barrier_semaphore()
    for by in range(1, REACH + 1):
        for sign in (1, -1):
            pl.semaphore_signal(barrier, inc=1, device_id=at(sign * by), device_id_type=MESH)

    @pl.when(t > 0)
    def _():
        pl.semaphore_signal(barrier, inc=1, device_id=down, device_id_type=MESH)

    @pl.when(t < nt - 1)
    def _():
        pl.semaphore_signal(barrier, inc=1, device_id=up, device_id_type=MESH)

    rows = jnp.concatenate([guess_ref[0, 0], guess_ref[0, 1], init_ref[0], init_ref[1]], axis=0)
    packed = permuted(rows, perm_matrix(True))
    halves[0] = packed[:, :128]
    halves[1] = packed[:, 128:]
    for plane in range(2):
        for row in range(2):
            for col in range(2):
                part = slice(64 * row + 32 * col, 64 * row + 32 * col + 32)
                g[2 + plane, part, :] = halves[col, pl.ds(64 * plane + row, 32, stride=2), :]
                q1[2 + plane, part, :] = halves[col, pl.ds(128 + 64 * plane + row, 32, stride=2), :]
    own = restricted(q1, 2)
    ic[REACH] = own

    @pl.when(t == 0)
    def _():
        f[2:4] = q1[2:4]
        f2[2:4] = q1[2:4]

    pl.semaphore_wait(barrier, 2 * REACH + jnp.where((t > 0) & (t < nt - 1), 2, 1))

    ids = iter(range(200))

    def message(src, dst, number, device):
        return pltpu.make_async_remote_copy(
            src_ref=src, dst_ref=dst, send_sem=ssem.at[number], recv_sem=rsem.at[number],
            device_id=device, device_id_type=MESH,
        )

    def start(copies):
        for copy in copies:
            copy.start()

    def arrive(copies):
        for copy in copies:
            copy.wait_recv()

    def sent(copies):
        for copy in copies:
            copy.wait_send()

    def halo(ref):
        return [
            message(ref.at[pl.ds(2, 2)], ref.at[pl.ds(0, 2)], next(ids), at(1)),
            message(ref.at[pl.ds(2, 2)], ref.at[pl.ds(4, 2)], next(ids), at(-1)),
        ]

    def spread(ref, middle, far, near=1):
        out = []
        for by in range(near, far + 1):
            for sign in (1, -1):
                out.append(message(ref.at[middle], ref.at[middle - sign * by], next(ids), at(sign * by)))
        return out

    ic_near = spread(ic, REACH, 5)
    ic_mid = spread(ic, REACH, 7, 6)
    ic_far = spread(ic, REACH, 9, 8)
    g_up = message(g.at[pl.ds(2, 2)], f.at[pl.ds(2, 2)], next(ids), up)
    g_halo = halo(g)
    f_halo = halo(f)
    v_near = spread(v, DEEP, 3)
    v_far = spread(v, DEEP, 5, 4)
    n1_halo = halo(n1)
    n2_halo = halo(n2)
    n2_up = message(n2.at[pl.ds(2, 2)], f2.at[pl.ds(2, 2)], next(ids), up)
    f2_halo = halo(f2)
    s_core = message(t2.at[pl.ds(2, 7)], s.at[pl.ds(2, 7)], next(ids), up)
    s_cross = message(t2.at[DEEP], s.at[DEEP], next(ids), up)
    s_spread = spread(s, DEEP, 5)

    @pl.when(t < nt - 1)
    def _():
        g_up.start()

    start(ic_near)

    @pl.when(t >= 2)
    def _():
        start(ic_mid)

    @pl.when(t == 3)
    def _():
        start(ic_far)

    start(g_halo)

    @pl.when(t == 0)
    def _():
        start(f_halo)

    @pl.when(lax.rem(t, 2) == 1)
    def _():
        g_up.wait_recv()
        start(f_halo)

    arrive(ic_near)

    @pl.when(t >= 2)
    def _():
        arrive(ic_mid)

    @pl.when(t == 3)
    def _():
        arrive(ic_far)

    @pl.when(t < 2)
    def _():
        for j in (*range(REACH - 5), *range(REACH + 6, 2 * REACH + 1)):
            ic[j] = own

    @pl.when(t == 2)
    def _():
        for j in (0, 1, 2 * REACH - 1, 2 * REACH):
            ic[j] = own

    for j in range(2 * REACH + 1):
        sa[j] = ic[j]

    sb[0] = own
    sb[2 * REACH] = own

    def two_steps(_, carry):
        for j in range(1, 2 * REACH):
            sb[j] = euler(sa[j - 1], sa[j], sa[j + 1])
        for j in range(2, 2 * REACH - 1):
            sa[j] = euler(sb[j - 1], sb[j], sb[j + 1])
        return carry

    lax.fori_loop(0, t, two_steps, 0)
    for j in range(REACH - 2, REACH + 3):
        sb[j] = euler(sa[j - 1], sa[j], sa[j + 1])
    for j in range(3):
        k = REACH - 1 + j
        w[0, j] = sa[k]
        w[1, j] = sb[k]
        w[2, j] = euler(sb[k - 1], sb[k], sb[k + 1])

    @pl.when(t == 2)
    def _():
        g_up.wait_recv()
        start(f_halo)

    arrive(g_halo)
    arrive(f_halo)
    old = [restricted(g, 2 * j) for j in range(3)]
    shifts = [[w[m, j] - old[j] for j in range(3)] for m in range(3)]
    fine_sweep((g, g, g), shifts, f, z1, z2, q1, q2, d2, n1, 2, n2, 2)

    v[DEEP, 0] = restricted(f, 2)
    v[DEEP, 1] = restricted(n1, 2)
    v[DEEP, 2] = restricted(n2, 2)
    start(v_near)

    @pl.when(even)
    def _():
        start(v_far)

    @pl.when(t < nt - 1)
    def _():
        n2_up.start()

    start(n1_halo)
    start(n2_halo)

    @pl.when(t == 0)
    def _():
        f2[0:2] = f[0:2]
        f2[4:6] = f[4:6]
        for j in range(2 * DEEP + 1):
            s[j] = ic[REACH - DEEP + j]

    @pl.when(lax.rem(t, 2) == 1)
    def _():
        n2_up.wait_recv()
        start(f2_halo)

    arrive(v_near)

    @pl.when(even)
    def _():
        arrive(v_far)

    def forcing(weights, out, j):
        z = [mix(weights, [v[k, m] for m in range(3)]) for k in (j - 1, j, j + 1)]
        cubes = mix(weights, [cube(v[j, m]) for m in range(3)])
        out[j] = 0.25 * coarse_sum(*z) - 0.5 * z[1] - cubes

    def forcings(reach):
        for j in range(DEEP - reach, DEEP + reach + 1):
            forcing(A, c1, j)
            if abs(j - DEEP) < reach:
                forcing(B, c2, j)

    def chain(reach):
        for j in range(DEEP - reach, DEEP + reach + 1):
            t1[j] = euler(s[j - 1], s[j], s[j + 1]) + c1[j]
        for j in range(DEEP - reach + 1, DEEP + reach):
            t2[j] = euler(t1[j - 1], t1[j], t1[j + 1]) + c2[j]

    @pl.when(even)
    def _():
        forcings(4)

    @pl.when(jnp.logical_not(even))
    def _():
        forcings(2)

    @pl.when(t == 2)
    def _():
        n2_up.wait_recv()
        start(f2_halo)
        s_cross.wait_recv()
        start(s_spread)
        arrive(s_spread)

    @pl.when(even)
    def _():
        chain(4)
        s_core.start()

    @pl.when(jnp.logical_not(even))
    def _():
        s_core.wait_recv()
        chain(2)

    @pl.when(t == 1)
    def _():
        s_cross.start()

    arrive(n1_halo)
    arrive(n2_halo)

    @pl.when(t > 0)
    def _():
        arrive(f2_halo)

    shifts = []
    for m, level in enumerate((s, t1, t2)):
        shifts.append([level[DEEP - 1 + j] - v[DEEP - 1 + j, m] for j in range(3)])
    fine_sweep((f, n1, n2), shifts, f2, z1, z2, q1, q2, d2, None, 0, out_ref, 0)

    sent(ic_near)
    sent(g_halo)
    sent(f_halo)
    sent(v_near)
    sent(n1_halo)
    sent(n2_halo)

    @pl.when(t >= 2)
    def _():
        sent(ic_mid)

    @pl.when(t == 3)
    def _():
        sent(ic_far)

    @pl.when(t < nt - 1)
    def _():
        g_up.wait_send()
        n2_up.wait_send()

    @pl.when(t > 0)
    def _():
        sent(f2_halo)

    @pl.when(even)
    def _():
        sent(v_far)
        s_core.wait_send()

    @pl.when(t == 1)
    def _():
        s_cross.wait_send()

    @pl.when(t == 2)
    def _():
        sent(s_spread)


def interleave(x_ref, out_ref, halves):
    for plane in range(2):
        for row in range(2):
            for col in range(2):
                halves[col, pl.ds(64 * plane + row, 32, stride=2), :] = sub(x_ref, plane, 2 * row + col)
    wide = permuted(jnp.concatenate([halves[0], halves[1]], axis=1), perm_matrix(False))
    out_ref[0, 0] = wide[:64]
    out_ref[0, 1] = wide[64:]


def solution(mesh):
    ns, nt = mesh.shape["space"], mesh.shape["tm"]
    vmem = pl.BlockSpec(memory_space=pltpu.VMEM)

    def local(initial, guess):
        slab6 = pltpu.VMEM((6, 128, 128), jnp.float32)

        def planes(*lead):
            return pltpu.VMEM((*lead, 32, 128), jnp.float32)

        last = pl.pallas_call(
            functools.partial(kernel, ns, nt),
            out_shape=jax.ShapeDtypeStruct((2, 128, 128), jnp.float32),
            in_specs=[vmem, vmem],
            out_specs=vmem,
            scratch_shapes=[slab6] * 10
            + [planes(2 * REACH + 1)] * 3
            + [planes(3, 3), planes(2 * DEEP + 1, 3)]
            + [planes(2 * DEEP + 1)] * 5
            + [pltpu.VMEM((2, 256, 128), jnp.float32)]
            + [pltpu.SemaphoreType.DMA((64,)), pltpu.SemaphoreType.DMA((64,))],
            compiler_params=pltpu.CompilerParams(
                collective_id=0, has_side_effects=True, vmem_limit_bytes=32 << 20
            ),
            name="pfasst",
        )(initial, guess)
        return pl.pallas_call(
            interleave,
            out_shape=jax.ShapeDtypeStruct(guess.shape, jnp.float32),
            in_specs=[vmem],
            out_specs=vmem,
            scratch_shapes=[pltpu.VMEM((2, 128, 128), jnp.float32)],
            compiler_params=pltpu.CompilerParams(vmem_limit_bytes=32 << 20),
            name="interleave",
        )(last)

    return jax.shard_map(
        local,
        mesh=mesh,
        in_specs=(P("space", None, None), P("tm", "space", None, None)),
        out_specs=P("tm", "space", None, None),
        check_vma=False,
    )
```

```python
import functools

import jax
import jax.numpy as jnp
from jax import lax
from jax.experimental import pallas as pl
from jax.experimental.pallas import tpu as pltpu
from jax.sharding import PartitionSpec as P

MESH = pl.DeviceIdType.MESH
DT, H = 0.24, 0.12
A = (DT * 5.0 / 24.0 - H, DT / 3.0, -DT / 24.0)
B = (-DT / 24.0, DT / 3.0 - H, DT * 5.0 / 24.0)
REACH = 9
DEEP = 5


def split(x):
    high = x.astype(jnp.bfloat16)
    rest = x - high.astype(jnp.float32)
    mid = rest.astype(jnp.bfloat16)
    low = (rest - mid.astype(jnp.float32)).astype(jnp.bfloat16)
    return jnp.concatenate([high, mid, low], axis=0)


def permuted(x, perm):
    rows = x.shape[0]
    out = jnp.dot(split(x), perm, preferred_element_type=jnp.float32)
    return out[:rows] + (out[rows : 2 * rows] + out[2 * rows :])


def perm_matrix(to_parity):
    i = lax.broadcasted_iota(jnp.int32, (256, 256), 0)
    j = lax.broadcasted_iota(jnp.int32, (256, 256), 1)
    wide, packed = (i, j) if to_parity else (j, i)
    lane = jnp.where(packed < 128, 2 * packed, 2 * packed - 255)
    return jnp.where(wide == lane, 1.0, 0.0).astype(jnp.bfloat16)


def lane_roll(x, by):
    return pltpu.roll(x, by % 128, 1)


def row_roll(x, by):
    return pltpu.roll(x, by % 32, 0)


def coarse_sum(below, x, above):
    total = below + above
    total = total + lane_roll(x, 1) + lane_roll(x, -1)
    return total + row_roll(x, 1) + row_roll(x, -1)


def euler(below, x, above):
    return 0.25 * H * coarse_sum(below, x, above) + x * ((1.0 - 0.5 * H) - H * (x * x))


def cube(x):
    return x * x * x


def mix(weights, values):
    return weights[0] * values[0] + weights[1] * values[1] + weights[2] * values[2]


def sub(ref, plane, part):
    return ref[plane, 32 * part : 32 * part + 32, :]


def restricted(ref, first):
    total = None
    for plane in (first, first + 1):
        for part in range(4):
            piece = sub(ref, plane, part)
            total = piece if total is None else total + piece
    return 0.125 * total


def fine_sum(ref, plane, part):
    row, col = part // 2, part % 2
    beside = sub(ref, plane, row * 2 + 1 - col)
    over = sub(ref, plane, (1 - row) * 2 + col)
    total = sub(ref, plane - 1, part) + sub(ref, plane + 1, part)
    total = total + beside + lane_roll(beside, 1 if col == 0 else -1)
    return total + over + row_roll(over, 1 if row == 0 else -1)


def fine_sweep(nodes, shifts, start, z1, z2, q1, q2, d2, out1, first1, out2, first2):
    for plane in range(6):
        for part in range(4):
            rows = slice(32 * part, 32 * part + 32)
            u = [sub(nodes[m], plane, part) + shifts[m][plane // 2] for m in range(3)]
            n0 = sub(start, plane, part)
            z = H * n0 + mix(A, u)
            z1[plane, rows, :] = z
            if 1 <= plane <= 4:
                cubes = [cube(v) for v in u]
                q1[plane, rows, :] = n0 - 5.0 * z - (H * cube(n0) + mix(A, cubes))
                d2[plane, rows, :] = mix(B, u)
                if 2 <= plane <= 3:
                    q2[plane, rows, :] = mix(B, cubes)
    for plane in range(1, 5):
        for part in range(4):
            rows = slice(32 * part, 32 * part + 32)
            n1 = sub(q1, plane, part) + fine_sum(z1, plane, part)
            z = H * n1 + sub(d2, plane, part)
            z2[plane, rows, :] = z
            if 2 <= plane <= 3:
                if out1 is not None:
                    out1[first1 + plane - 2, rows, :] = n1
                q2[plane, rows, :] = n1 - 5.0 * z - (H * cube(n1) + sub(q2, plane, part))
    for plane in range(2, 4):
        for part in range(4):
            rows = slice(32 * part, 32 * part + 32)
            out2[first2 + plane - 2, rows, :] = sub(q2, plane, part) + fine_sum(z2, plane, part)


def when(cond, body):
    if cond is None:
        body()
    else:
        pl.when(cond)(body)


class Group:
    def __init__(self, copies, sends=None, receives=None, far=None):
        self.copies, self.sends, self.receives, self.far = copies, sends, receives, far


def kernel(
    ns, nt,
    init_ref, guess_ref, out_ref,
    raw, g, f, n1, n2, f2, i6,
    z1, z2, q1, q2, d2,
    ic, sa, sb, w, v, va, c1, c2, s, t1, t2, halves,
    ssem, rsem, lsem, answer,
):
    t = lax.axis_index("tm")
    c = lax.axis_index("space")
    even = lax.rem(t, 2) == 0
    odd = jnp.logical_not(even)
    low = t < 2
    high = t >= 2
    opposite = lax.rem(t + 2, nt)

    loads = [
        pltpu.make_async_copy(guess_ref.at[0], raw.at[pl.ds(0, 2)], lsem.at[0]),
        pltpu.make_async_copy(init_ref, raw.at[pl.ds(2, 2)], lsem.at[1]),
    ]
    for load in loads:
        load.start()

    def wraps(by):
        return (c + by >= ns) if by > 0 else (c + by < 0)

    def at(by, row=None):
        return (t if row is None else row, lax.rem(c + by + ns, ns))

    up = (jnp.minimum(t + 1, nt - 1), c)
    down = (jnp.maximum(t - 1, 0), c)

    barrier = pltpu.get_barrier_semaphore()
    expected, answers, replies = 0, [0, 0], []

    def signal(semaphore, device):
        pl.semaphore_signal(semaphore, inc=1, device_id=device, device_id_type=MESH)

    def link(sends, receives, source):
        nonlocal expected
        when(receives, lambda: signal(barrier, source))
        expected = expected + (1 if sends is None else jnp.where(sends, 1, 0))

    def far(kind, early, to_late, late, to_early):
        nonlocal expected
        pl.when(early)(lambda: signal(barrier, to_late))
        expected = expected + jnp.where(late, 1, 0)
        answers[kind] = answers[kind] + jnp.where(early, 1, 0)
        replies.append((kind, late, to_early))

    both = [sign * by for by in range(1, REACH + 1) for sign in (1, -1)]
    link(even, odd, down)
    link(odd, even, up)
    far(1, t == 1, up, t == 2, down)
    for by in both:
        if abs(by) <= DEEP:
            link(high | ~wraps(by), high | ~wraps(-by), at(-by))
            link(high & wraps(by), low & wraps(-by), at(-by, opposite))
            far(1, (t == 1) & wraps(by), at(by, 2), (t == 2) & wraps(-by), at(-by, 1))
        else:
            sender = (even if by > 0 else odd) & high
            link(sender, sender, at(-by))
        if -DEEP <= by < 0:
            far(0, low & wraps(by), at(by), low & wraps(-by), at(-by))

    for load in loads:
        load.wait()
    packed = permuted(jnp.concatenate([raw[k] for k in range(4)], axis=0), perm_matrix(True))
    halves[0] = packed[:, :128]
    halves[1] = packed[:, 128:]
    for plane in range(2):
        for row in range(2):
            for col in range(2):
                part = slice(64 * row + 32 * col, 64 * row + 32 * col + 32)
                g[2 + plane, part, :] = halves[col, pl.ds(64 * plane + row, 32, stride=2), :]
                i6[2 + plane, part, :] = halves[col, pl.ds(128 + 64 * plane + row, 32, stride=2), :]
    own = restricted(i6, 2)
    ic[REACH] = own

    @pl.when(t == 0)
    def _():
        f[2:4] = i6[2:4]
        f2[2:4] = i6[2:4]
        for j in range(REACH - DEEP):
            ic[j] = own

    @pl.when(t == 1)
    def _():
        for j in range(REACH + DEEP + 1, 2 * REACH + 1):
            ic[j] = own

    pl.semaphore_wait(barrier, expected)
    for kind, late, to_early in replies:
        pl.when(late)(functools.partial(signal, answer.at[kind], to_early))

    ids = iter(range(200))
    launched, arrived = [], []

    def message(src, dst, device):
        number = next(ids)
        return pltpu.make_async_remote_copy(
            src_ref=src, dst_ref=dst, send_sem=ssem.at[number], recv_sem=rsem.at[number],
            device_id=device, device_id_type=MESH,
        )

    def launch(*groups):
        for group in groups:
            launched.append(group)

            def body(group=group):
                for copy in group.copies:
                    copy.start()

            when(group.sends, body)

    def arrive(*groups):
        for group in groups:
            arrived.append(group)

            def body(group=group):
                for copy in group.copies:
                    copy.wait_recv()

            when(group.receives, body)

    def drain(groups):
        for group in groups:

            def body(group=group):
                for copy in group.copies:
                    copy.wait_send()

            when(group.sends, body)

    def slab(ref, side=0):
        return ref.at[pl.ds(2 + 2 * side, 2)]

    def halo(ref, sends=None, receives=None):
        return Group([message(slab(ref), slab(ref, -1), at(1)), message(slab(ref), slab(ref, 1), at(-1))], sends, receives)

    def spread(ref, middle, reaches, sends=None):
        out = []
        for by in reaches:
            out.append(message(ref.at[middle], ref.at[middle - by], at(by)))
        return Group(out, sends, sends)

    def chunk(ref, k, side=0):
        return ref.at[2 + k // 2 + 2 * side, pl.ds(64 * (k % 2), 64)]

    def crossing(src, dst):
        return [Group([message(chunk(src, k), chunk(dst, k), up)], t == 1, t == 2) for k in range(4)]

    def chunked_halo(ref):
        return [
            [
                Group([message(chunk(ref, k), chunk(ref, k, -by), at(by))], (t == 2) & ~wraps(by), (t == 2) & ~wraps(-by))
                for by in (1, -1)
            ]
            for k in range(4)
        ]

    def around(src, dst):
        return [
            Group([message(slab(src), slab(dst, -by), at(by, 2))], (t == 1) & wraps(by), (t == 2) & wraps(-by))
            for by in (1, -1)
        ]

    def sides(src, dst):
        return Group([message(slab(src, k), slab(dst, k), up) for k in (-1, 1)], even, odd)

    g_cross = crossing(g, f)
    g_halo = [
        Group([message(slab(g), slab(g, -1), at(1))]),
        Group([message(slab(g), slab(g, 1), at(-1))], high | ~wraps(-1), None, low & wraps(-1)),
    ]
    g_core = Group([message(slab(g), slab(f), up)], even, odd)
    g_sides = sides(g, f)
    i_halo = []
    for by in (1, -1):
        row = jnp.where(wraps(by), 0, t)
        copy = message(slab(i6), slab(f, -by), at(by, row))
        i_halo.append(Group([copy], (t == 0) & ~wraps(by) | (t == 2) & wraps(by), t == 0))
    f_halo = chunked_halo(f)
    f_around = around(g, f)
    ic_halo = []
    for by in both:
        sender = even if by > 0 else odd
        if abs(by) > DEEP:
            ic_halo.append(Group([message(ic.at[REACH], ic.at[REACH - by], at(by))], sender & high, sender & high))
            continue
        ic_halo.append(Group([message(ic.at[REACH], ic.at[REACH - by], at(by))], sender & (high | ~wraps(by)), sender & (high | ~wraps(-by))))
        copy = message(ic.at[REACH], ic.at[REACH - by], at(by, opposite))
        ic_halo.append(Group([copy], sender & high & wraps(by), sender & low & wraps(-by)))
    ic_swap = [
        Group([message(ic.at[pl.ds(0, REACH)], ic.at[pl.ds(0, REACH)], up)], even, odd),
        Group([message(ic.at[pl.ds(REACH + 1, REACH)], ic.at[pl.ds(REACH + 1, REACH)], down)], odd, even),
    ]
    v_halo, v0_odd, v0_two = [], [], []
    for by in both[:10]:
        nodes, sums = (v.at[DEEP, pl.ds(1, 2)], v.at[DEEP - by, pl.ds(1, 2)]), (va, v.at[DEEP - by, 1])
        starts = (v.at[DEEP, 0], v.at[DEEP - by, 0])
        far = abs(by)
        if far <= 2:
            v_halo.append(Group([message(*nodes, at(by))]))
            v0_odd.append(Group([message(*starts, at(by))], odd, odd))
        elif far < DEEP:
            v_halo.append(Group([message(*nodes, at(by))], even, even))
        if far == 3:
            v_halo.append(Group([message(*sums, at(by))], odd, odd))
        if far < DEEP:
            v0_two.append(Group([message(*starts, at(by))], t == 2, t == 2))
        else:
            v_halo.append(Group([message(*sums, at(by))], even, even))
    n1_halo = halo(n1)
    n2_halo = halo(n2)
    n2_cross = crossing(n2, f2)
    n2_core = Group([message(slab(n2), slab(f2), up)], even, odd)
    n2_sides = sides(n2, f2)
    f2_halo = chunked_halo(f2)
    f2_around = around(n2, f2)
    s_core = Group([message(t2.at[pl.ds(2, 7)], s.at[pl.ds(2, 7)], up)], even, odd)
    s_cross = Group([message(t2.at[DEEP], s.at[DEEP], up)], t == 1, t == 2)
    s_wrapped, s_spread = [], []
    for by in both[:10]:
        number = next(ids)
        for groups, src, sends in ((s_wrapped, t2, (t == 1) & wraps(by)), (s_spread, s, (t == 2) & ~wraps(by))):
            copy = pltpu.make_async_remote_copy(
                src_ref=src.at[DEEP], dst_ref=s.at[DEEP - by], send_sem=ssem.at[number], recv_sem=rsem.at[number],
                device_id=at(by, 2), device_id_type=MESH,
            )
            groups.append(Group([copy], sends, t == 2))

    launch(*ic_halo)
    launch(*g_halo)
    launch(g_core)
    launch(*i_halo)

    pl.when(answers[0] > 0)(lambda: pl.semaphore_wait(answer.at[0], answers[0]))
    launch(*(Group(x.copies, x.far) for x in (*ic_halo, *g_halo) if x.far is not None))

    arrive(g_core)

    @pl.when(odd)
    def _():
        v[DEEP, 0] = restricted(f, 2)

    launch(*v0_odd)

    edge = (c < DEEP) | (c >= ns - DEEP)

    def cross(here):
        pl.when((t == 1) & here)(lambda: pl.semaphore_wait(answer.at[1], answers[1]))
        launch(*(Group(x.copies, x.sends & here) for x in (*g_cross, *f_around)))

    cross(edge)

    arrive(*ic_halo)
    launch(*ic_swap)
    arrive(*ic_swap)

    for j in range(2 * REACH + 1):
        sa[j] = ic[j]

    sb[0] = own
    sb[2 * REACH] = own

    def two_steps(_, carry):
        for j in range(1, 2 * REACH):
            sb[j] = euler(sa[j - 1], sa[j], sa[j + 1])
        for j in range(2, 2 * REACH - 1):
            sa[j] = euler(sb[j - 1], sb[j], sb[j + 1])
        return carry

    lax.fori_loop(0, t, two_steps, 0)
    for j in range(REACH - 2, REACH + 3):
        sb[j] = euler(sa[j - 1], sa[j], sa[j + 1])
    for j in range(3):
        k = REACH - 1 + j
        w[0, j] = sa[k]
        w[1, j] = sb[k]
        w[2, j] = euler(sb[k - 1], sb[k], sb[k + 1])

    arrive(*g_halo)
    launch(g_sides)

    arrive(g_sides, *i_halo)
    for crossed, passed in zip(g_cross, f_halo):
        arrive(crossed)
        launch(*passed)

    @pl.when(t == 2)
    def _():
        v[DEEP, 0] = restricted(f, 2)

    @pl.when(t == 0)
    def _():
        for j in range(2 * DEEP + 1):
            v[j, 0] = ic[REACH - DEEP + j]

    launch(*v0_two)
    for passed in f_halo:
        arrive(*passed)
    arrive(*f_around)

    old = [restricted(g, 2 * j) for j in range(3)]
    shifts = [[w[m, j] - old[j] for j in range(3)] for m in range(3)]
    fine_sweep((g, g, g), shifts, f, z1, z2, q1, q2, d2, n1, 2, n2, 2)

    first = list(launched)
    v[DEEP, 1] = restricted(n1, 2)
    v[DEEP, 2] = restricted(n2, 2)
    va[...] = mix(A, [v[DEEP, m] for m in range(3)])
    launch(*v_halo)
    launch(n2_core)
    cross(~edge)

    n_halo = [n1_halo, n2_halo]
    launch(*(Group(x.copies, high & edge) for x in n_halo))
    arrive(s_cross)
    launch(*s_spread)
    launch(*(Group(x.copies, high & ~edge) for x in n_halo))
    drain(first)
    arrive(*v0_odd, *v0_two, *v_halo)
    launch(*(Group(x.copies, low) for x in n_halo))

    def forcing(weights, out, j, sums=()):
        z = [v[k, 1] if k in sums else mix(weights, [v[k, m] for m in range(3)]) for k in (j - 1, j, j + 1)]
        cubes = mix(weights, [cube(v[j, m]) for m in range(3)])
        out[j] = 0.25 * coarse_sum(*z) - 0.5 * z[1] - cubes

    def forcings(reach):
        for j in range(DEEP - reach, DEEP + reach + 1):
            forcing(A, c1, j, (DEEP - reach - 1, DEEP + reach + 1))
            if abs(j - DEEP) < reach:
                forcing(B, c2, j)

    def chain(reach):
        for j in range(DEEP - reach, DEEP + reach + 1):
            t1[j] = euler(s[j - 1], s[j], s[j + 1]) + c1[j]
        for j in range(DEEP - reach + 1, DEEP + reach):
            t2[j] = euler(t1[j - 1], t1[j], t1[j + 1]) + c2[j]

    when(even, lambda: forcings(4))
    when(odd, lambda: forcings(2))

    @pl.when(t == 0)
    def _():
        f2[0:2] = f[0:2]
        f2[4:6] = f[4:6]
        for j in range(2 * DEEP + 1):
            s[j] = ic[REACH - DEEP + j]

    for crossed, passed in zip(n2_cross, f2_halo):
        arrive(crossed)
        launch(*passed)

    arrive(*s_spread)

    when(even, lambda: chain(4))
    launch(s_core)
    arrive(s_core)
    when(odd, lambda: chain(2))
    launch(s_cross)
    launch(*s_wrapped)
    launch(*n2_cross, *f2_around)

    arrive(n2_halo)
    launch(n2_sides)

    arrive(n1_halo, n2_core, n2_sides, *f2_around)
    for passed in f2_halo:
        arrive(*passed)

    shifts = []
    for m, level in enumerate((s, t1, t2)):
        shifts.append([level[DEEP - 1 + j] - v[DEEP - 1 + j, m] for j in range(3)])
    fine_sweep((f, n1, n2), shifts, f2, z1, z2, q1, q2, d2, None, 0, out_ref, 0)

    drain(launched[len(first) :])


def interleave(x_ref, out_ref, halves):
    for plane in range(2):
        for row in range(2):
            for col in range(2):
                halves[col, pl.ds(64 * plane + row, 32, stride=2), :] = sub(x_ref, plane, 2 * row + col)
    wide = permuted(jnp.concatenate([halves[0], halves[1]], axis=1), perm_matrix(False))
    out_ref[0, 0] = wide[:64]
    out_ref[0, 1] = wide[64:]


def solution(mesh):
    ns, nt = mesh.shape["space"], mesh.shape["tm"]
    vmem = pl.BlockSpec(memory_space=pltpu.VMEM)

    def local(initial, guess):
        slab6 = pltpu.VMEM((6, 128, 128), jnp.float32)

        def planes(*lead):
            return pltpu.VMEM((*lead, 32, 128), jnp.float32)

        last = pl.pallas_call(
            functools.partial(kernel, ns, nt),
            out_shape=pltpu.VMEM((2, 128, 128), jnp.float32),
            in_specs=[pl.BlockSpec(memory_space=pltpu.HBM)] * 2,
            out_specs=vmem,
            scratch_shapes=[pltpu.VMEM((4, 64, 256), jnp.float32)]
            + [slab6] * 11
            + [planes(2 * REACH + 1)] * 3
            + [planes(3, 3), planes(2 * DEEP + 1, 3), planes()]
            + [planes(2 * DEEP + 1)] * 5
            + [pltpu.VMEM((2, 256, 128), jnp.float32)]
            + [pltpu.SemaphoreType.DMA((160,))] * 2
            + [pltpu.SemaphoreType.DMA((2,)), pltpu.SemaphoreType.REGULAR((2,))],
            compiler_params=pltpu.CompilerParams(
                collective_id=0, has_side_effects=True, vmem_limit_bytes=32 << 20
            ),
            name="pfasst",
        )(*(pltpu.with_memory_space_constraint(x, pltpu.HBM) for x in (initial, guess)))
        return pl.pallas_call(
            interleave,
            out_shape=jax.ShapeDtypeStruct(guess.shape, jnp.float32),
            in_specs=[vmem],
            out_specs=vmem,
            scratch_shapes=[pltpu.VMEM((2, 128, 128), jnp.float32)],
            compiler_params=pltpu.CompilerParams(vmem_limit_bytes=32 << 20),
            name="interleave",
        )(last)

    return jax.shard_map(
        local,
        mesh=mesh,
        in_specs=(P("space", None, None), P("tm", "space", None, None)),
        out_specs=P("tm", "space", None, None),
        check_vma=False,
    )
```

```python
import functools

import jax
import jax.numpy as jnp
from jax import lax
from jax.experimental import pallas as pl
from jax.experimental.pallas import tpu as pltpu
from jax.sharding import PartitionSpec as P

MESH = pl.DeviceIdType.MESH
DT, H = 0.24, 0.12
A = (DT * 5.0 / 24.0 - H, DT / 3.0, -DT / 24.0)
B = (-DT / 24.0, DT / 3.0 - H, DT * 5.0 / 24.0)
REACH = 9
DEEP = 5


def split(x):
    high = x.astype(jnp.bfloat16)
    rest = x - high.astype(jnp.float32)
    mid = rest.astype(jnp.bfloat16)
    low = (rest - mid.astype(jnp.float32)).astype(jnp.bfloat16)
    return jnp.concatenate([high, mid, low], axis=0)


def permuted(x, perm):
    rows = x.shape[0]
    out = jnp.dot(split(x), perm, preferred_element_type=jnp.float32)
    return out[:rows] + (out[rows : 2 * rows] + out[2 * rows :])


def perm_matrix(to_parity):
    i = lax.broadcasted_iota(jnp.int32, (256, 256), 0)
    j = lax.broadcasted_iota(jnp.int32, (256, 256), 1)
    wide, packed = (i, j) if to_parity else (j, i)
    lane = jnp.where(packed < 128, 2 * packed, 2 * packed - 255)
    return jnp.where(wide == lane, 1.0, 0.0).astype(jnp.bfloat16)


def lane_roll(x, by):
    return pltpu.roll(x, by % 128, 1)


def row_roll(x, by):
    return pltpu.roll(x, by % 32, 0)


def coarse_sum(below, x, above):
    total = below + above
    total = total + lane_roll(x, 1) + lane_roll(x, -1)
    return total + row_roll(x, 1) + row_roll(x, -1)


def euler(below, x, above):
    return 0.25 * H * coarse_sum(below, x, above) + x * ((1.0 - 0.5 * H) - H * (x * x))


def cube(x):
    return x * x * x


def mix(weights, values):
    return weights[0] * values[0] + weights[1] * values[1] + weights[2] * values[2]


def sub(ref, plane, part):
    return ref[plane, 32 * part : 32 * part + 32, :]


def restricted(ref, first):
    total = None
    for plane in (first, first + 1):
        for part in range(4):
            piece = sub(ref, plane, part)
            total = piece if total is None else total + piece
    return 0.125 * total


def fine_sum(ref, plane, part):
    row, col = part // 2, part % 2
    beside = sub(ref, plane, row * 2 + 1 - col)
    over = sub(ref, plane, (1 - row) * 2 + col)
    total = sub(ref, plane - 1, part) + sub(ref, plane + 1, part)
    total = total + beside + lane_roll(beside, 1 if col == 0 else -1)
    return total + over + row_roll(over, 1 if row == 0 else -1)


def fine_sweep(nodes, shifts, start, z1, z2, q1, q2, d2, out1, first1, out2, first2):
    for plane in range(6):
        for part in range(4):
            rows = slice(32 * part, 32 * part + 32)
            u = [sub(nodes[m], plane, part) + shifts[m][plane // 2] for m in range(3)]
            n0 = sub(start, plane, part)
            z = H * n0 + mix(A, u)
            z1[plane, rows, :] = z
            if 1 <= plane <= 4:
                cubes = [cube(v) for v in u]
                q1[plane, rows, :] = n0 - 5.0 * z - (H * cube(n0) + mix(A, cubes))
                d2[plane, rows, :] = mix(B, u)
                if 2 <= plane <= 3:
                    q2[plane, rows, :] = mix(B, cubes)
    for plane in range(1, 5):
        for part in range(4):
            rows = slice(32 * part, 32 * part + 32)
            n1 = sub(q1, plane, part) + fine_sum(z1, plane, part)
            z = H * n1 + sub(d2, plane, part)
            z2[plane, rows, :] = z
            if 2 <= plane <= 3:
                if out1 is not None:
                    out1[first1 + plane - 2, rows, :] = n1
                q2[plane, rows, :] = n1 - 5.0 * z - (H * cube(n1) + sub(q2, plane, part))
    for plane in range(2, 4):
        for part in range(4):
            rows = slice(32 * part, 32 * part + 32)
            out2[first2 + plane - 2, rows, :] = sub(q2, plane, part) + fine_sum(z2, plane, part)


IC, SWAP, GUESS, CORE, SIDES, STARTS, NODES, N1, N2, CORE2, SIDES2, CROSS, SPREAD, PAIR, A_CHUNK, B_CHUNK = range(16)
CHUNKS = 4


def kernel(
    ns, nt,
    init_ref, guess_ref, out_ref,
    raw, g, f, n1, n2, f2, i6,
    z1, z2, q1, q2, d2,
    ic, sa, sb, w, v, va, c1, c2, s, t1, t2, halves,
    ssem, rsem, lsem, answer, passed,
):
    t = lax.axis_index("tm")
    c = lax.axis_index("space")
    even = lax.rem(t, 2) == 0
    odd = lax.rem(t, 2) == 1
    low, high = t < 2, t >= 2
    opposite = lax.rem(t + 2, nt)
    middle = (c >= REACH) & (c < ns - REACH)
    outer = (c < REACH) | (c >= ns - REACH)
    edge = (c < DEEP) | (c >= ns - DEEP)
    inland = (c >= DEEP) & (c < ns - DEEP)

    loads = [
        pltpu.make_async_copy(guess_ref.at[0], raw.at[pl.ds(0, 2)], lsem.at[0]),
        pltpu.make_async_copy(init_ref, raw.at[pl.ds(2, 2)], lsem.at[1]),
    ]
    for load in loads:
        load.start()

    def wraps(by):
        return (c + by >= ns) if by > 0 else (c + by < 0)

    def at(by, row=None):
        return (t if row is None else row, lax.rem(c + by + ns, ns))

    up = (jnp.minimum(t + 1, nt - 1), c)
    down = (jnp.maximum(t - 1, 0), c)

    barrier = pltpu.get_barrier_semaphore()
    row = jnp.minimum(t, 2)

    def signal(semaphore, device):
        pl.semaphore_signal(semaphore, inc=1, device_id=device, device_id_type=MESH)

    near = [sign * by for by in range(1, DEEP + 1) for sign in (1, -1)]

    @pl.when(edge)
    def _():
        for by in near:

            @pl.when(wraps(by))
            def _(by=by):
                signal(barrier, at(by, row))
                pl.when(low)(lambda: signal(barrier, at(by, 2)))
                pl.when(t == 1)(lambda: signal(barrier, at(by, 3)))

    pl.when(even)(lambda: signal(barrier, up))
    pl.when(odd)(lambda: signal(barrier, down))
    pl.when(t == 1)(lambda: signal(barrier, (3, c)))
    for by in near:
        pl.when(jnp.logical_not(wraps(by)))(lambda by=by: signal(barrier, at(by, row)))

    @pl.when(high & even)
    def _():
        for by in range(DEEP + 1, REACH + 1):
            signal(barrier, at(-by))

    @pl.when(high & odd)
    def _():
        for by in range(DEEP + 1, REACH + 1):
            signal(barrier, at(by, 2))

    around = 0
    for by in near:
        around = around + jnp.where(wraps(by), 1, 0)
    count = len(near)
    expected = jnp.where(low, count + 1, jnp.where(t == 2, 2 * count + 2 * (REACH - DEEP) + 1 + 2 * around, 2 + around))

    for load in loads:
        load.wait()
    packed = permuted(jnp.concatenate([raw[k] for k in range(4)], axis=0), perm_matrix(True))
    halves[0] = packed[:, :128]
    halves[1] = packed[:, 128:]
    for plane in range(2):
        for row in range(2):
            for col in range(2):
                part = slice(64 * row + 32 * col, 64 * row + 32 * col + 32)
                g[2 + plane, part, :] = halves[col, pl.ds(64 * plane + row, 32, stride=2), :]
                i6[2 + plane, part, :] = halves[col, pl.ds(128 + 64 * plane + row, 32, stride=2), :]
    own = restricted(i6, 2)
    ic[REACH] = own

    @pl.when(t == 0)
    def _():
        f[2:4] = i6[2:4]
        f2[2:4] = i6[2:4]
        for j in range(REACH - DEEP):
            ic[j] = own

    @pl.when(t == 1)
    def _():
        for j in range(REACH + DEEP + 1, 2 * REACH + 1):
            ic[j] = own

    pl.semaphore_wait(barrier, expected)

    @pl.when(t == 3)
    def _():
        signal(answer, (1, c))

        @pl.when(edge)
        def _():
            for by in near:
                pl.when(wraps(by))(lambda by=by: signal(answer, at(by, 1)))

        pl.semaphore_wait(passed, 1)

    @pl.when(t == 2)
    def _():
        signal(passed, up)

    ids = iter(range(200))
    launched = []

    def message(src, dst, number, device):
        return pltpu.make_async_remote_copy(
            src_ref=src, dst_ref=dst, send_sem=ssem.at[next(ids)], recv_sem=rsem.at[number],
            device_id=device, device_id_type=MESH,
        )

    def each(sends, items, act):
        if all(wrapped is None for _, wrapped in items):

            @pl.when(sends)
            def _():
                for copy, _ in items:
                    act(copy)

            return
        inner = [copy for copy, wrapped in items if wrapped is None or not wrapped[1]]
        if inner:

            @pl.when(sends & middle)
            def _():
                for copy in inner:
                    act(copy)

        @pl.when(sends & outer)
        def _():
            for copy, wrapped in items:
                if wrapped is None:
                    act(copy)
                elif wrapped[1]:
                    pl.when(wraps(wrapped[0]))(functools.partial(act, copy))
                else:
                    pl.when(jnp.logical_not(wraps(wrapped[0])))(functools.partial(act, copy))

    def launch(sends, items):
        launched.append((sends, items))
        each(sends, items, lambda copy: copy.start())

    def drain(groups):
        for sends, items in groups:
            each(sends, items, lambda copy: copy.wait_send())

    def landed(ref, number):
        pltpu.make_async_remote_copy(
            src_ref=ref, dst_ref=ref, send_sem=ssem.at[0], recv_sem=rsem.at[number],
            device_id=up, device_id_type=MESH,
        ).wait_recv()

    always = t >= 0

    def slab(ref, side=0):
        return ref.at[pl.ds(2 + 2 * side, 2)]

    def slabs(ref):
        return ref.at[pl.ds(0, 4)]

    def halo(ref, number):
        return [(message(slab(ref), slab(ref, -by), number, at(by)), None) for by in (1, -1)]

    def chunk(ref, k, side=0):
        return ref.at[2 + k // 2 + 2 * side, pl.ds(64 * (k % 2), 64)]

    def crossing(src, dst, number, sides):
        out = [(message(chunk(src, k), chunk(dst, k), number + 2 * k, up), None) for k in range(CHUNKS)]
        return out + [(message(slab(src), slab(dst, -by), sides, at(by, 2)), (by, True)) for by in (1, -1)]

    def forward(ref, k, number):
        return [(message(chunk(ref, k), chunk(ref, k, -by), number, at(by)), (by, False)) for by in (1, -1)]

    def sides(src, dst, number):
        return [(message(slab(src, k), slab(dst, k), number, up), None) for k in (-1, 1)]

    def plane(by, device, wrapped):
        return (message(ic.at[REACH], ic.at[REACH - by], IC, device), wrapped)

    for sender, sign in ((even, 1), (odd, -1)):
        offsets = [sign * by for by in range(1, REACH + 1)]
        launch(sender & low, [plane(by, at(by), (by, False)) for by in offsets[:DEEP]])
        launch(
            sender & high,
            [plane(by, at(by), None) for by in offsets]
            + [plane(by, at(by, opposite), (by, True)) for by in offsets[:DEEP]],
        )
    launch(always, halo(g, GUESS))
    launch(even, [(message(slab(g), slab(f), CORE, up), None)])
    launch(t == 0, [(message(slab(i6), slab(f, -by), SIDES, at(by)), (by, False)) for by in (1, -1)])
    launch(t == 2, [(message(slab(i6), slab(f, -by), SIDES, at(by, 0)), (by, True)) for by in (1, -1)])

    def start_planes(reach):
        return [
            (message(v.at[DEEP, 0], v.at[DEEP - sign * by, 0], STARTS, at(sign * by)), None)
            for by in range(1, reach + 1) for sign in (1, -1)
        ]

    @pl.when(odd)
    def _():
        landed(slab(f), CORE)
        v[DEEP, 0] = restricted(f, 2)

    launch(odd, start_planes(2))

    answers = 1 + around
    crossed = crossing(g, f, A_CHUNK, SIDES)

    @pl.when((t == 1) & edge)
    def _():
        pl.semaphore_wait(answer, answers)

    launch((t == 1) & edge, crossed)

    @pl.when(even)
    def _():
        pl.when(low)(lambda: landed(ic.at[pl.ds(REACH - DEEP, DEEP)], IC))
        pl.when(high)(lambda: landed(ic.at[pl.ds(0, REACH)], IC))

    @pl.when(odd)
    def _():
        pl.when(low)(lambda: landed(ic.at[pl.ds(REACH + 1, DEEP)], IC))
        pl.when(high)(lambda: landed(ic.at[pl.ds(REACH + 1, REACH)], IC))

    left, right = ic.at[pl.ds(0, REACH)], ic.at[pl.ds(REACH + 1, REACH)]
    launch(even, [(message(left, left, SWAP, up), None)])
    launch(odd, [(message(right, right, SWAP, down), None)])
    pl.when(even)(lambda: landed(right, SWAP))
    pl.when(odd)(lambda: landed(left, SWAP))

    for j in range(2 * REACH + 1):
        sa[j] = ic[j]

    sb[0] = own
    sb[2 * REACH] = own

    def two_steps(_, carry):
        for j in range(1, 2 * REACH):
            sb[j] = euler(sa[j - 1], sa[j], sa[j + 1])
        for j in range(2, 2 * REACH - 1):
            sa[j] = euler(sb[j - 1], sb[j], sb[j + 1])
        return carry

    lax.fori_loop(0, t, two_steps, 0)
    for j in range(REACH - 2, REACH + 3):
        sb[j] = euler(sa[j - 1], sa[j], sa[j + 1])
    for j in range(3):
        k = REACH - 1 + j
        w[0, j] = sa[k]
        w[1, j] = sb[k]
        w[2, j] = euler(sb[k - 1], sb[k], sb[k + 1])

    landed(slabs(g), GUESS)
    launch(even, sides(g, f, SIDES))

    for k in range(CHUNKS):
        pl.when(t == 2)(lambda k=k: landed(chunk(f, k), A_CHUNK + 2 * k))
        launch(t == 2, forward(f, k, SIDES))

    @pl.when(t == 2)
    def _():
        v[DEEP, 0] = restricted(f, 2)

    @pl.when(t == 0)
    def _():
        for j in range(2 * DEEP + 1):
            v[j, 0] = ic[REACH - DEEP + j]

    launch(t == 2, start_planes(4))
    landed(slabs(f), SIDES)

    old = [restricted(g, 2 * j) for j in range(3)]
    shifts = [[w[m, j] - old[j] for j in range(3)] for m in range(3)]
    fine_sweep((g, g, g), shifts, f, z1, z2, q1, q2, d2, n1, 2, n2, 2)

    first = list(launched)
    v[DEEP, 1] = restricted(n1, 2)
    v[DEEP, 2] = restricted(n2, 2)
    va[...] = mix(A, [v[DEEP, m] for m in range(3)])

    def node_planes(by):
        return (message(v.at[DEEP, pl.ds(1, 2)], v.at[DEEP - by, pl.ds(1, 2)], NODES, at(by)), None)

    def sum_plane(by):
        return (message(va, v.at[DEEP - by, 1], NODES, at(by)), None)

    launch(even, [node_planes(by) for by in near[:8]] + [sum_plane(by) for by in near[8:]])
    launch(odd, [node_planes(by) for by in near[:4]] + [sum_plane(by) for by in near[4:6]])
    launch(even, [(message(slab(n2), slab(f2), CORE2, up), None)])

    @pl.when((t == 1) & inland)
    def _():
        pl.semaphore_wait(answer, answers)

    launch((t == 1) & inland, crossed)

    n_halo = halo(n2, N2) + halo(n1, N1)
    launch(high & edge, n_halo)
    pl.when(t == 2)(lambda: landed(s.at[DEEP], CROSS))
    launch(
        t == 2,
        [(message(s.at[DEEP], s.at[DEEP - by], SPREAD, at(by)), (by, False)) for by in near],
    )
    launch(high & inland, n_halo)
    drain(first)

    @pl.when(even)
    def _():
        pl.when(high)(lambda: landed(v.at[pl.ds(0, 8), 0], STARTS))
        landed(v.at[pl.ds(0, 6)], NODES)

    @pl.when(odd)
    def _():
        landed(v.at[pl.ds(0, 4), 0], STARTS)
        landed(v.at[pl.ds(0, 5), pl.ds(1, 2)], NODES)

    launch(low, n_halo)

    for k in range(CHUNKS):
        pl.when(t == 2)(lambda k=k: landed(chunk(f2, k), B_CHUNK + 2 * k))
        launch(t == 2, forward(f2, k, SIDES2))

    def forcing(weights, out, j, sums=()):
        z = [v[k, 1] if k in sums else mix(weights, [v[k, m] for m in range(3)]) for k in (j - 1, j, j + 1)]
        cubes = mix(weights, [cube(v[j, m]) for m in range(3)])
        out[j] = 0.25 * coarse_sum(*z) - 0.5 * z[1] - cubes

    def forcings(reach):
        for j in range(DEEP - reach, DEEP + reach + 1):
            forcing(A, c1, j, (DEEP - reach - 1, DEEP + reach + 1))
            if abs(j - DEEP) < reach:
                forcing(B, c2, j)

    def chain(reach):
        for j in range(DEEP - reach, DEEP + reach + 1):
            t1[j] = euler(s[j - 1], s[j], s[j + 1]) + c1[j]
        for j in range(DEEP - reach + 1, DEEP + reach):
            t2[j] = euler(t1[j - 1], t1[j], t1[j + 1]) + c2[j]

    pl.when(even)(lambda: forcings(4))
    pl.when(odd)(lambda: forcings(2))

    @pl.when(t == 0)
    def _():
        f2[0:2] = f[0:2]
        f2[4:6] = f[4:6]
        for j in range(2 * DEEP + 1):
            s[j] = ic[REACH - DEEP + j]

    pl.when(t == 2)(lambda: landed(s.at[pl.ds(0, 10)], SPREAD))

    pl.when(even)(lambda: chain(4))
    launch(even, [(message(t2.at[pl.ds(2, 7)], s.at[pl.ds(2, 7)], PAIR, up), None)])

    @pl.when(odd)
    def _():
        landed(s.at[pl.ds(2, 7)], PAIR)
        chain(2)

    launch(
        t == 1,
        [(message(t2.at[DEEP], s.at[DEEP], CROSS, up), None)]
        + [(message(t2.at[DEEP], s.at[DEEP - by], SPREAD, at(by, 2)), (by, True)) for by in near],
    )
    crossed = crossing(n2, f2, B_CHUNK, SIDES2)
    launch((t == 1) & edge, crossed)

    landed(slabs(n2), N2)
    launch(even, sides(n2, f2, SIDES2))
    landed(slabs(n1), N1)
    launch((t == 1) & inland, crossed)

    pl.when(odd)(lambda: landed(slab(f2), CORE2))
    pl.when(t > 0)(lambda: landed(slabs(f2), SIDES2))

    shifts = []
    for m, level in enumerate((s, t1, t2)):
        shifts.append([level[DEEP - 1 + j] - v[DEEP - 1 + j, m] for j in range(3)])
    fine_sweep((f, n1, n2), shifts, f2, z1, z2, q1, q2, d2, None, 0, out_ref, 0)

    drain(launched[len(first) :])


def interleave(x_ref, out_ref, halves):
    for plane in range(2):
        for row in range(2):
            for col in range(2):
                halves[col, pl.ds(64 * plane + row, 32, stride=2), :] = sub(x_ref, plane, 2 * row + col)
    wide = permuted(jnp.concatenate([halves[0], halves[1]], axis=1), perm_matrix(False))
    out_ref[0, 0] = wide[:64]
    out_ref[0, 1] = wide[64:]


def solution(mesh):
    ns, nt = mesh.shape["space"], mesh.shape["tm"]
    vmem = pl.BlockSpec(memory_space=pltpu.VMEM)

    def local(initial, guess):
        slab6 = pltpu.VMEM((6, 128, 128), jnp.float32)

        def planes(*lead):
            return pltpu.VMEM((*lead, 32, 128), jnp.float32)

        last = pl.pallas_call(
            functools.partial(kernel, ns, nt),
            out_shape=pltpu.VMEM((2, 128, 128), jnp.float32),
            in_specs=[pl.BlockSpec(memory_space=pltpu.HBM)] * 2,
            out_specs=vmem,
            scratch_shapes=[pltpu.VMEM((4, 64, 256), jnp.float32)]
            + [slab6] * 11
            + [planes(2 * REACH + 1)] * 3
            + [planes(3, 3), planes(2 * DEEP + 1, 3), planes()]
            + [planes(2 * DEEP + 1)] * 5
            + [pltpu.VMEM((2, 256, 128), jnp.float32)]
            + [pltpu.SemaphoreType.DMA((160,)), pltpu.SemaphoreType.DMA((24,))]
            + [pltpu.SemaphoreType.DMA((2,)), pltpu.SemaphoreType.REGULAR, pltpu.SemaphoreType.REGULAR],
            compiler_params=pltpu.CompilerParams(
                collective_id=0, has_side_effects=True, vmem_limit_bytes=32 << 20
            ),
            name="pfasst",
        )(*(pltpu.with_memory_space_constraint(x, pltpu.HBM) for x in (initial, guess)))
        return pl.pallas_call(
            interleave,
            out_shape=jax.ShapeDtypeStruct(guess.shape, jnp.float32),
            in_specs=[vmem],
            out_specs=vmem,
            scratch_shapes=[pltpu.VMEM((2, 128, 128), jnp.float32)],
            compiler_params=pltpu.CompilerParams(vmem_limit_bytes=32 << 20),
            name="interleave",
        )(last)

    return jax.shard_map(
        local,
        mesh=mesh,
        in_specs=(P("space", None, None), P("tm", "space", None, None)),
        out_specs=P("tm", "space", None, None),
        check_vma=False,
    )
```

```python
import functools

import jax
import jax.numpy as jnp
from jax import lax
from jax.experimental import pallas as pl
from jax.experimental.pallas import tpu as pltpu
from jax.sharding import PartitionSpec as P

MESH = pl.DeviceIdType.MESH
DT, H = 0.24, 0.12
A = (DT * 5.0 / 24.0 - H, DT / 3.0, -DT / 24.0)
B = (-DT / 24.0, DT / 3.0 - H, DT * 5.0 / 24.0)
REACH = 9
DEEP = 5


def split(x):
    high = x.astype(jnp.bfloat16)
    rest = x - high.astype(jnp.float32)
    mid = rest.astype(jnp.bfloat16)
    low = (rest - mid.astype(jnp.float32)).astype(jnp.bfloat16)
    return jnp.concatenate([high, mid, low], axis=0)


def permuted(x, perm):
    rows = x.shape[0]
    out = jnp.dot(split(x), perm, preferred_element_type=jnp.float32)
    return out[:rows] + (out[rows : 2 * rows] + out[2 * rows :])


def perm_matrix(to_parity):
    i = lax.broadcasted_iota(jnp.int32, (256, 256), 0)
    j = lax.broadcasted_iota(jnp.int32, (256, 256), 1)
    wide, packed = (i, j) if to_parity else (j, i)
    lane = jnp.where(packed < 128, 2 * packed, 2 * packed - 255)
    return jnp.where(wide == lane, 1.0, 0.0).astype(jnp.bfloat16)


def lane_roll(x, by):
    return pltpu.roll(x, by % 128, 1)


def row_roll(x, by):
    return pltpu.roll(x, by % 32, 0)


def coarse_sum(below, x, above):
    total = below + above
    total = total + lane_roll(x, 1) + lane_roll(x, -1)
    return total + row_roll(x, 1) + row_roll(x, -1)


def euler(below, x, above):
    return 0.25 * H * coarse_sum(below, x, above) + x * ((1.0 - 0.5 * H) - H * (x * x))


def cube(x):
    return x * x * x


def mix(weights, values):
    return weights[0] * values[0] + weights[1] * values[1] + weights[2] * values[2]


def sub(ref, plane, part):
    return ref[plane, 32 * part : 32 * part + 32, :]


def restricted(ref, first):
    total = None
    for plane in (first, first + 1):
        for part in range(4):
            piece = sub(ref, plane, part)
            total = piece if total is None else total + piece
    return 0.125 * total


def fine_sum(ref, plane, part):
    row, col = part // 2, part % 2
    beside = sub(ref, plane, row * 2 + 1 - col)
    over = sub(ref, plane, (1 - row) * 2 + col)
    total = sub(ref, plane - 1, part) + sub(ref, plane + 1, part)
    total = total + beside + lane_roll(beside, 1 if col == 0 else -1)
    return total + over + row_roll(over, 1 if row == 0 else -1)


def fine_sweep(nodes, shifts, start, z1, z2, q1, q2, d2, out1, first1, out2, first2):
    for plane in range(6):
        for part in range(4):
            rows = slice(32 * part, 32 * part + 32)
            u = [sub(nodes[m], plane, part) + shifts[m][plane // 2] for m in range(3)]
            n0 = sub(start, plane, part)
            z = H * n0 + mix(A, u)
            z1[plane, rows, :] = z
            if 1 <= plane <= 4:
                cubes = [cube(v) for v in u]
                q1[plane, rows, :] = n0 - 5.0 * z - (H * cube(n0) + mix(A, cubes))
                d2[plane, rows, :] = mix(B, u)
                if 2 <= plane <= 3:
                    q2[plane, rows, :] = mix(B, cubes)
    for plane in range(1, 5):
        for part in range(4):
            rows = slice(32 * part, 32 * part + 32)
            n1 = sub(q1, plane, part) + fine_sum(z1, plane, part)
            z = H * n1 + sub(d2, plane, part)
            z2[plane, rows, :] = z
            if 2 <= plane <= 3:
                if out1 is not None:
                    out1[first1 + plane - 2, rows, :] = n1
                q2[plane, rows, :] = n1 - 5.0 * z - (H * cube(n1) + sub(q2, plane, part))
    for plane in range(2, 4):
        for part in range(4):
            rows = slice(32 * part, 32 * part + 32)
            out2[first2 + plane - 2, rows, :] = sub(q2, plane, part) + fine_sum(z2, plane, part)


IC, SWAP, GUESS, CORE, SIDES, STARTS, NODES, N1, N2, CORE2, SIDES2, CROSS, SPREAD, PAIR, A_CHUNK, B_CHUNK = range(16)
CHUNKS = 4


def kernel(
    ns, nt,
    init_ref, guess_ref, out_ref,
    raw, g, f, n1, n2, f2, i6,
    z1, z2, q1, q2, d2,
    ic, sa, sb, w, v, va, c1, c2, s, t1, t2, halves,
    ssem, rsem, lsem, answer, passed,
):
    t = lax.axis_index("tm")
    c = lax.axis_index("space")
    even = lax.rem(t, 2) == 0
    odd = lax.rem(t, 2) == 1
    low, high = t < 2, t >= 2
    opposite = lax.rem(t + 2, nt)
    middle = (c >= REACH) & (c < ns - REACH)
    outer = (c < REACH) | (c >= ns - REACH)
    edge = (c < DEEP) | (c >= ns - DEEP)
    soon = (c < DEEP) | (c >= 3 * ns // 4)
    later = (c >= DEEP) & (c < 3 * ns // 4)
    inland = (c >= DEEP) & (c < ns - DEEP)

    loads = [
        pltpu.make_async_copy(guess_ref.at[0], raw.at[pl.ds(0, 2)], lsem.at[0]),
        pltpu.make_async_copy(init_ref, raw.at[pl.ds(2, 2)], lsem.at[1]),
    ]
    for load in loads:
        load.start()

    def wraps(by):
        return (c + by >= ns) if by > 0 else (c + by < 0)

    def at(by, row=None):
        return (t if row is None else row, lax.rem(c + by + ns, ns))

    up = (jnp.minimum(t + 1, nt - 1), c)
    down = (jnp.maximum(t - 1, 0), c)

    barrier = pltpu.get_barrier_semaphore()
    row = jnp.minimum(t, 2)

    def signal(semaphore, device):
        pl.semaphore_signal(semaphore, inc=1, device_id=device, device_id_type=MESH)

    near = [sign * by for by in range(1, DEEP + 1) for sign in (1, -1)]

    @pl.when(edge)
    def _():
        for by in near:

            @pl.when(wraps(by))
            def _(by=by):
                signal(barrier, at(by, row))
                pl.when(low)(lambda: signal(barrier, at(by, 2)))
                pl.when(t == 1)(lambda: signal(barrier, at(by, 3)))

    pl.when(even)(lambda: signal(barrier, up))
    pl.when(odd)(lambda: signal(barrier, down))
    pl.when(t == 1)(lambda: signal(barrier, (3, c)))
    for by in near:
        pl.when(jnp.logical_not(wraps(by)))(lambda by=by: signal(barrier, at(by, row)))

    @pl.when(high & even)
    def _():
        for by in range(DEEP + 1, REACH + 1):
            signal(barrier, at(-by))

    @pl.when(high & odd)
    def _():
        for by in range(DEEP + 1, REACH + 1):
            signal(barrier, at(by, 2))

    around = 0
    for by in near:
        around = around + jnp.where(wraps(by), 1, 0)
    count = len(near)
    expected = jnp.where(low, count + 1, jnp.where(t == 2, 2 * count + 2 * (REACH - DEEP) + 1 + 2 * around, 2 + around))

    for load in loads:
        load.wait()
    packed = permuted(jnp.concatenate([raw[k] for k in range(4)], axis=0), perm_matrix(True))
    halves[0] = packed[:, :128]
    halves[1] = packed[:, 128:]
    for plane in range(2):
        for row in range(2):
            for col in range(2):
                part = slice(64 * row + 32 * col, 64 * row + 32 * col + 32)
                g[2 + plane, part, :] = halves[col, pl.ds(64 * plane + row, 32, stride=2), :]
                i6[2 + plane, part, :] = halves[col, pl.ds(128 + 64 * plane + row, 32, stride=2), :]
    own = restricted(i6, 2)
    ic[REACH] = own

    @pl.when(t == 0)
    def _():
        f[2:4] = i6[2:4]
        f2[2:4] = i6[2:4]
        for j in range(REACH - DEEP):
            ic[j] = own

    @pl.when(t == 1)
    def _():
        for j in range(REACH + DEEP + 1, 2 * REACH + 1):
            ic[j] = own

    pl.semaphore_wait(barrier, expected)

    @pl.when(t == 3)
    def _():
        signal(answer, (1, c))

        @pl.when(edge)
        def _():
            for by in near:
                pl.when(wraps(by))(lambda by=by: signal(answer, at(by, 1)))

        pl.semaphore_wait(passed, 1)

    @pl.when(t == 2)
    def _():
        signal(passed, up)

    ids = iter(range(200))
    launched = []

    def message(src, dst, number, device):
        return pltpu.make_async_remote_copy(
            src_ref=src, dst_ref=dst, send_sem=ssem.at[next(ids)], recv_sem=rsem.at[number],
            device_id=device, device_id_type=MESH,
        )

    def each(sends, items, act):
        if all(wrapped is None for _, wrapped in items):

            @pl.when(sends)
            def _():
                for copy, _ in items:
                    act(copy)

            return
        inner = [copy for copy, wrapped in items if wrapped is None or not wrapped[1]]
        if inner:

            @pl.when(sends & middle)
            def _():
                for copy in inner:
                    act(copy)

        @pl.when(sends & outer)
        def _():
            for copy, wrapped in items:
                if wrapped is None:
                    act(copy)
                elif wrapped[1]:
                    pl.when(wraps(wrapped[0]))(functools.partial(act, copy))
                else:
                    pl.when(jnp.logical_not(wraps(wrapped[0])))(functools.partial(act, copy))

    def launch(sends, items):
        launched.append((sends, items))
        each(sends, items, lambda copy: copy.start())

    def drain(groups):
        for sends, items in groups:
            each(sends, items, lambda copy: copy.wait_send())

    def landed(ref, number):
        pltpu.make_async_remote_copy(
            src_ref=ref, dst_ref=ref, send_sem=ssem.at[0], recv_sem=rsem.at[number],
            device_id=up, device_id_type=MESH,
        ).wait_recv()

    always = t >= 0

    def slab(ref, side=0):
        return ref.at[pl.ds(2 + 2 * side, 2)]

    def slabs(ref):
        return ref.at[pl.ds(0, 4)]

    def halo(ref, number):
        return [(message(slab(ref), slab(ref, -by), number, at(by)), None) for by in (1, -1)]

    def chunk(ref, k, side=0):
        return ref.at[2 + k // 2 + 2 * side, pl.ds(64 * (k % 2), 64)]

    def crossing(src, dst, number, sides):
        out = [(message(chunk(src, k), chunk(dst, k), number + 2 * k, up), None) for k in range(CHUNKS)]
        return out + [(message(slab(src), slab(dst, -by), sides, at(by, 2)), (by, True)) for by in (1, -1)]

    def forward(ref, k, number):
        return [(message(chunk(ref, k), chunk(ref, k, -by), number, at(by)), (by, False)) for by in (1, -1)]

    def sides(src, dst, number):
        return [(message(slab(src, k), slab(dst, k), number, up), None) for k in (-1, 1)]

    def plane(by, device, wrapped):
        return (message(ic.at[REACH], ic.at[REACH - by], IC, device), wrapped)

    for sender, sign in ((even, 1), (odd, -1)):
        offsets = [sign * by for by in range(1, REACH + 1)]
        launch(sender & low, [plane(by, at(by), (by, False)) for by in offsets[:DEEP]])
        launch(
            sender & high,
            [plane(by, at(by), None) for by in offsets]
            + [plane(by, at(by, opposite), (by, True)) for by in offsets[:DEEP]],
        )
    launch(always, halo(g, GUESS))
    launch(even, [(message(slab(g), slab(f), CORE, up), None)])
    launch(t == 0, [(message(slab(i6), slab(f, -by), SIDES, at(by)), (by, False)) for by in (1, -1)])
    launch(t == 2, [(message(slab(i6), slab(f, -by), SIDES, at(by, 0)), (by, True)) for by in (1, -1)])

    def start_planes(reach):
        return [
            (message(v.at[DEEP, 0], v.at[DEEP - sign * by, 0], STARTS, at(sign * by)), None)
            for by in range(1, reach + 1) for sign in (1, -1)
        ]

    @pl.when(odd)
    def _():
        landed(slab(f), CORE)
        v[DEEP, 0] = restricted(f, 2)

    launch(odd, start_planes(2))

    answers = 1 + around
    crossed = crossing(g, f, A_CHUNK, SIDES)

    @pl.when((t == 1) & soon)
    def _():
        pl.semaphore_wait(answer, answers)

    launch((t == 1) & soon, crossed)

    @pl.when(even)
    def _():
        pl.when(low)(lambda: landed(ic.at[pl.ds(REACH - DEEP, DEEP)], IC))
        pl.when(high)(lambda: landed(ic.at[pl.ds(0, REACH)], IC))

    @pl.when(odd)
    def _():
        pl.when(low)(lambda: landed(ic.at[pl.ds(REACH + 1, DEEP)], IC))
        pl.when(high)(lambda: landed(ic.at[pl.ds(REACH + 1, REACH)], IC))

    left, right = ic.at[pl.ds(0, REACH)], ic.at[pl.ds(REACH + 1, REACH)]
    launch(even, [(message(left, left, SWAP, up), None)])
    launch(odd, [(message(right, right, SWAP, down), None)])
    pl.when(even)(lambda: landed(right, SWAP))
    pl.when(odd)(lambda: landed(left, SWAP))

    for j in range(2 * REACH + 1):
        sa[j] = ic[j]

    sb[0] = own
    sb[2 * REACH] = own

    def two_steps(_, carry):
        for j in range(1, 2 * REACH):
            sb[j] = euler(sa[j - 1], sa[j], sa[j + 1])
        for j in range(2, 2 * REACH - 1):
            sa[j] = euler(sb[j - 1], sb[j], sb[j + 1])
        return carry

    lax.fori_loop(0, t, two_steps, 0)
    for j in range(REACH - 2, REACH + 3):
        sb[j] = euler(sa[j - 1], sa[j], sa[j + 1])
    for j in range(3):
        k = REACH - 1 + j
        w[0, j] = sa[k]
        w[1, j] = sb[k]
        w[2, j] = euler(sb[k - 1], sb[k], sb[k + 1])

    landed(slabs(g), GUESS)
    launch(even, sides(g, f, SIDES))

    for k in range(CHUNKS):
        pl.when(t == 2)(lambda k=k: landed(chunk(f, k), A_CHUNK + 2 * k))
        launch(t == 2, forward(f, k, SIDES))

    @pl.when(t == 2)
    def _():
        v[DEEP, 0] = restricted(f, 2)

    @pl.when(t == 0)
    def _():
        for j in range(2 * DEEP + 1):
            v[j, 0] = ic[REACH - DEEP + j]

    launch(t == 2, start_planes(4))
    landed(slabs(f), SIDES)

    old = [restricted(g, 2 * j) for j in range(3)]
    shifts = [[w[m, j] - old[j] for j in range(3)] for m in range(3)]
    fine_sweep((g, g, g), shifts, f, z1, z2, q1, q2, d2, n1, 2, n2, 2)

    first = list(launched)
    v[DEEP, 1] = restricted(n1, 2)
    v[DEEP, 2] = restricted(n2, 2)
    va[...] = mix(A, [v[DEEP, m] for m in range(3)])

    def node_planes(by):
        return (message(v.at[DEEP, pl.ds(1, 2)], v.at[DEEP - by, pl.ds(1, 2)], NODES, at(by)), None)

    def sum_plane(by):
        return (message(va, v.at[DEEP - by, 1], NODES, at(by)), None)

    launch(even, [node_planes(by) for by in near[:8]] + [sum_plane(by) for by in near[8:]])
    launch(odd, [node_planes(by) for by in near[:4]] + [sum_plane(by) for by in near[4:6]])
    launch(even, [(message(slab(n2), slab(f2), CORE2, up), None)])

    @pl.when((t == 1) & later)
    def _():
        pl.semaphore_wait(answer, answers)

    launch((t == 1) & later, crossed)

    n_halo = halo(n2, N2) + halo(n1, N1)
    launch(high & edge, n_halo)
    n_inner = [(copy, (by, False)) for (copy, _), by in zip(n_halo, (1, -1, 1, -1))]
    n_around = [(copy, (by, True)) for (copy, _), by in zip(n_halo, (1, -1, 1, -1))]
    launch(low & edge, n_inner)
    launch(low & (c == ns - 1), n_around)
    pl.when(t == 2)(lambda: landed(s.at[DEEP], CROSS))
    launch(
        t == 2,
        [(message(s.at[DEEP], s.at[DEEP - by], SPREAD, at(by)), (by, False)) for by in near],
    )
    launch(high & inland, n_halo)
    drain(first)

    @pl.when(even)
    def _():
        pl.when(high)(lambda: landed(v.at[pl.ds(0, 8), 0], STARTS))
        landed(v.at[pl.ds(0, 6)], NODES)

    @pl.when(odd)
    def _():
        landed(v.at[pl.ds(0, 4), 0], STARTS)
        landed(v.at[pl.ds(0, 5), pl.ds(1, 2)], NODES)


    crossed = crossing(n2, f2, B_CHUNK, SIDES2)
    launch((t == 1) & later, crossed)

    for k in range(CHUNKS):
        pl.when(t == 2)(lambda k=k: landed(chunk(f2, k), B_CHUNK + 2 * k))
        launch(t == 2, forward(f2, k, SIDES2))

    def forcing(weights, out, j, sums=()):
        z = [v[k, 1] if k in sums else mix(weights, [v[k, m] for m in range(3)]) for k in (j - 1, j, j + 1)]
        cubes = mix(weights, [cube(v[j, m]) for m in range(3)])
        out[j] = 0.25 * coarse_sum(*z) - 0.5 * z[1] - cubes

    def forcings(reach):
        for j in range(DEEP - reach, DEEP + reach + 1):
            forcing(A, c1, j, (DEEP - reach - 1, DEEP + reach + 1))
            if abs(j - DEEP) < reach:
                forcing(B, c2, j)

    def chain(reach):
        for j in range(DEEP - reach, DEEP + reach + 1):
            t1[j] = euler(s[j - 1], s[j], s[j + 1]) + c1[j]
        for j in range(DEEP - reach + 1, DEEP + reach):
            t2[j] = euler(t1[j - 1], t1[j], t1[j + 1]) + c2[j]

    pl.when(even)(lambda: forcings(4))
    pl.when(odd)(lambda: forcings(2))

    @pl.when(t == 0)
    def _():
        f2[0:2] = f[0:2]
        f2[4:6] = f[4:6]
        for j in range(2 * DEEP + 1):
            s[j] = ic[REACH - DEEP + j]

    pl.when(t == 2)(lambda: landed(s.at[pl.ds(0, 10)], SPREAD))

    pl.when(even)(lambda: chain(4))
    launch(even, [(message(t2.at[pl.ds(2, 7)], s.at[pl.ds(2, 7)], PAIR, up), None)])

    @pl.when(odd)
    def _():
        landed(s.at[pl.ds(2, 7)], PAIR)
        chain(2)

    launch(
        t == 1,
        [(message(t2.at[DEEP], s.at[DEEP], CROSS, up), None)]
        + [(message(t2.at[DEEP], s.at[DEEP - by], SPREAD, at(by, 2)), (by, True)) for by in near],
    )
    launch((t == 1) & soon, crossed)

    launch(low & inland, n_halo)
    launch(low & (c == 0), n_around)

    landed(slabs(n2), N2)
    launch(even, sides(n2, f2, SIDES2))
    landed(slabs(n1), N1)

    pl.when(odd)(lambda: landed(slab(f2), CORE2))
    pl.when(t > 0)(lambda: landed(slabs(f2), SIDES2))

    shifts = []
    for m, level in enumerate((s, t1, t2)):
        shifts.append([level[DEEP - 1 + j] - v[DEEP - 1 + j, m] for j in range(3)])
    fine_sweep((f, n1, n2), shifts, f2, z1, z2, q1, q2, d2, None, 0, out_ref, 0)

    drain(launched[len(first) :])


def interleave(x_ref, out_ref, halves):
    for plane in range(2):
        for row in range(2):
            for col in range(2):
                halves[col, pl.ds(64 * plane + row, 32, stride=2), :] = sub(x_ref, plane, 2 * row + col)
    wide = permuted(jnp.concatenate([halves[0], halves[1]], axis=1), perm_matrix(False))
    out_ref[0, 0] = wide[:64]
    out_ref[0, 1] = wide[64:]


def solution(mesh):
    ns, nt = mesh.shape["space"], mesh.shape["tm"]
    vmem = pl.BlockSpec(memory_space=pltpu.VMEM)

    def local(initial, guess):
        slab6 = pltpu.VMEM((6, 128, 128), jnp.float32)

        def planes(*lead):
            return pltpu.VMEM((*lead, 32, 128), jnp.float32)

        last = pl.pallas_call(
            functools.partial(kernel, ns, nt),
            out_shape=pltpu.VMEM((2, 128, 128), jnp.float32),
            in_specs=[pl.BlockSpec(memory_space=pltpu.HBM)] * 2,
            out_specs=vmem,
            scratch_shapes=[pltpu.VMEM((4, 64, 256), jnp.float32)]
            + [slab6] * 11
            + [planes(2 * REACH + 1)] * 3
            + [planes(3, 3), planes(2 * DEEP + 1, 3), planes()]
            + [planes(2 * DEEP + 1)] * 5
            + [pltpu.VMEM((2, 256, 128), jnp.float32)]
            + [pltpu.SemaphoreType.DMA((160,)), pltpu.SemaphoreType.DMA((24,))]
            + [pltpu.SemaphoreType.DMA((2,)), pltpu.SemaphoreType.REGULAR, pltpu.SemaphoreType.REGULAR],
            compiler_params=pltpu.CompilerParams(
                collective_id=0, has_side_effects=True, vmem_limit_bytes=32 << 20
            ),
            name="pfasst",
        )(*(pltpu.with_memory_space_constraint(x, pltpu.HBM) for x in (initial, guess)))
        return pl.pallas_call(
            interleave,
            out_shape=jax.ShapeDtypeStruct(guess.shape, jnp.float32),
            in_specs=[vmem],
            out_specs=vmem,
            scratch_shapes=[pltpu.VMEM((2, 128, 128), jnp.float32)],
            compiler_params=pltpu.CompilerParams(vmem_limit_bytes=32 << 20),
            name="interleave",
        )(last)

    return jax.shard_map(
        local,
        mesh=mesh,
        in_specs=(P("space", None, None), P("tm", "space", None, None)),
        out_specs=P("tm", "space", None, None),
        check_vma=False,
    )
```

```python
import functools

import jax
import jax.numpy as jnp
from jax import lax
from jax.experimental import pallas as pl
from jax.experimental.pallas import tpu as pltpu
from jax.sharding import PartitionSpec as P

MESH = pl.DeviceIdType.MESH
DT, H = 0.24, 0.12
A = (DT * 5.0 / 24.0 - H, DT / 3.0, -DT / 24.0)
B = (-DT / 24.0, DT / 3.0 - H, DT * 5.0 / 24.0)
REACH = 9
DEEP = 5


def split(x):
    high = x.astype(jnp.bfloat16)
    rest = x - high.astype(jnp.float32)
    mid = rest.astype(jnp.bfloat16)
    low = (rest - mid.astype(jnp.float32)).astype(jnp.bfloat16)
    return jnp.concatenate([high, mid, low], axis=0)


def permuted(x, perm):
    rows = x.shape[0]
    out = jnp.dot(split(x), perm, preferred_element_type=jnp.float32)
    return out[:rows] + (out[rows : 2 * rows] + out[2 * rows :])


def perm_matrix(to_parity):
    i = lax.broadcasted_iota(jnp.int32, (256, 256), 0)
    j = lax.broadcasted_iota(jnp.int32, (256, 256), 1)
    wide, packed = (i, j) if to_parity else (j, i)
    lane = jnp.where(packed < 128, 2 * packed, 2 * packed - 255)
    return jnp.where(wide == lane, 1.0, 0.0).astype(jnp.bfloat16)


def lane_roll(x, by):
    return pltpu.roll(x, by % 128, 1)


def row_roll(x, by):
    return pltpu.roll(x, by % 32, 0)


def coarse_sum(below, x, above):
    total = below + above
    total = total + lane_roll(x, 1) + lane_roll(x, -1)
    return total + row_roll(x, 1) + row_roll(x, -1)


def euler(below, x, above):
    return 0.25 * H * coarse_sum(below, x, above) + x * ((1.0 - 0.5 * H) - H * (x * x))


def cube(x):
    return x * x * x


def mix(weights, values):
    return weights[0] * values[0] + weights[1] * values[1] + weights[2] * values[2]


def sub(ref, plane, part):
    return ref[plane, 32 * part : 32 * part + 32, :]


def restricted(ref, first):
    total = None
    for plane in (first, first + 1):
        for part in range(4):
            piece = sub(ref, plane, part)
            total = piece if total is None else total + piece
    return 0.125 * total


def fine_sum(ref, plane, part):
    row, col = part // 2, part % 2
    beside = sub(ref, plane, row * 2 + 1 - col)
    over = sub(ref, plane, (1 - row) * 2 + col)
    total = sub(ref, plane - 1, part) + sub(ref, plane + 1, part)
    total = total + beside + lane_roll(beside, 1 if col == 0 else -1)
    return total + over + row_roll(over, 1 if row == 0 else -1)


def fine_sweep(nodes, shifts, start, z1, z2, q1, q2, d2, out1, first1, out2, first2):
    for plane in range(6):
        for part in range(4):
            rows = slice(32 * part, 32 * part + 32)
            u = [sub(nodes[m], plane, part) + shifts[m][plane // 2] for m in range(3)]
            n0 = sub(start, plane, part)
            z = H * n0 + mix(A, u)
            z1[plane, rows, :] = z
            if 1 <= plane <= 4:
                cubes = [cube(v) for v in u]
                q1[plane, rows, :] = n0 - 5.0 * z - (H * cube(n0) + mix(A, cubes))
                d2[plane, rows, :] = mix(B, u)
                if 2 <= plane <= 3:
                    q2[plane, rows, :] = mix(B, cubes)
    for plane in range(1, 5):
        for part in range(4):
            rows = slice(32 * part, 32 * part + 32)
            n1 = sub(q1, plane, part) + fine_sum(z1, plane, part)
            z = H * n1 + sub(d2, plane, part)
            z2[plane, rows, :] = z
            if 2 <= plane <= 3:
                if out1 is not None:
                    out1[first1 + plane - 2, rows, :] = n1
                q2[plane, rows, :] = n1 - 5.0 * z - (H * cube(n1) + sub(q2, plane, part))
    for plane in range(2, 4):
        for part in range(4):
            rows = slice(32 * part, 32 * part + 32)
            out2[first2 + plane - 2, rows, :] = sub(q2, plane, part) + fine_sum(z2, plane, part)


IC, SWAP, GUESS, CORE, SIDES, STARTS, NODES, N1, N2, CORE2, SIDES2, CROSS, SPREAD, PAIR, A_CHUNK, B_CHUNK = range(16)
CHUNKS = 4


def kernel(
    ns, nt,
    init_ref, guess_ref, out_ref,
    raw, g, f, n1, n2, f2, i6,
    z1, z2, q1, q2, d2,
    ic, sa, sb, w, v, va, c1, c2, s, t1, t2, halves,
    ssem, rsem, lsem, answer, passed,
):
    t = lax.axis_index("tm")
    c = lax.axis_index("space")
    even = lax.rem(t, 2) == 0
    odd = lax.rem(t, 2) == 1
    low, high = t < 2, t >= 2
    opposite = lax.rem(t + 2, nt)
    middle = (c >= REACH) & (c < ns - REACH)
    outer = (c < REACH) | (c >= ns - REACH)
    edge = (c < DEEP) | (c >= ns - DEEP)
    soon = (c < DEEP) | (c >= 3 * ns // 4)
    later = (c >= DEEP) & (c < 3 * ns // 4)
    inland = (c >= DEEP) & (c < ns - DEEP)

    loads = [
        pltpu.make_async_copy(guess_ref.at[0], raw.at[pl.ds(0, 2)], lsem.at[0]),
        pltpu.make_async_copy(init_ref, raw.at[pl.ds(2, 2)], lsem.at[1]),
    ]
    for load in loads:
        load.start()

    def wraps(by):
        return (c + by >= ns) if by > 0 else (c + by < 0)

    def at(by, row=None):
        return (t if row is None else row, lax.rem(c + by + ns, ns))

    up = (jnp.minimum(t + 1, nt - 1), c)
    down = (jnp.maximum(t - 1, 0), c)

    barrier = pltpu.get_barrier_semaphore()
    row = jnp.minimum(t, 2)

    def signal(semaphore, device):
        pl.semaphore_signal(semaphore, inc=1, device_id=device, device_id_type=MESH)

    near = [sign * by for by in range(1, DEEP + 1) for sign in (1, -1)]

    @pl.when(edge)
    def _():
        for by in near:

            @pl.when(wraps(by))
            def _(by=by):
                signal(barrier, at(by, row))
                pl.when(low)(lambda: signal(barrier, at(by, 2)))
                pl.when(t == 1)(lambda: signal(barrier, at(by, 3)))

    pl.when(even)(lambda: signal(barrier, up))
    pl.when(odd)(lambda: signal(barrier, down))
    pl.when(t == 1)(lambda: signal(barrier, (3, c)))
    for by in near:
        pl.when(jnp.logical_not(wraps(by)))(lambda by=by: signal(barrier, at(by, row)))

    @pl.when(high & even)
    def _():
        for by in range(DEEP + 1, REACH + 1):
            signal(barrier, at(-by))

    @pl.when(high & odd)
    def _():
        for by in range(DEEP + 1, REACH + 1):
            signal(barrier, at(by, 2))

    around = 0
    for by in near:
        around = around + jnp.where(wraps(by), 1, 0)
    count = len(near)
    expected = jnp.where(low, count + 1, jnp.where(t == 2, 2 * count + 2 * (REACH - DEEP) + 1 + 2 * around, 2 + around))

    for load in loads:
        load.wait()
    packed = permuted(jnp.concatenate([raw[k] for k in range(4)], axis=0), perm_matrix(True))
    halves[0] = packed[:, :128]
    halves[1] = packed[:, 128:]
    for plane in range(2):
        for row in range(2):
            for col in range(2):
                part = slice(64 * row + 32 * col, 64 * row + 32 * col + 32)
                g[2 + plane, part, :] = halves[col, pl.ds(64 * plane + row, 32, stride=2), :]
                i6[2 + plane, part, :] = halves[col, pl.ds(128 + 64 * plane + row, 32, stride=2), :]
    own = restricted(i6, 2)
    ic[REACH] = own

    @pl.when(t == 0)
    def _():
        f[2:4] = i6[2:4]
        f2[2:4] = i6[2:4]
        for j in range(REACH - DEEP):
            ic[j] = own

    @pl.when(t == 1)
    def _():
        for j in range(REACH + DEEP + 1, 2 * REACH + 1):
            ic[j] = own

    pl.semaphore_wait(barrier, expected)

    @pl.when(t == 3)
    def _():
        signal(answer, (1, c))

        @pl.when(edge)
        def _():
            for by in near:
                pl.when(wraps(by))(lambda by=by: signal(answer, at(by, 1)))

        pl.semaphore_wait(passed, 1)

    @pl.when(t == 2)
    def _():
        signal(passed, up)

    ids = iter(range(200))
    launched = []

    def message(src, dst, number, device):
        return pltpu.make_async_remote_copy(
            src_ref=src, dst_ref=dst, send_sem=ssem.at[next(ids)], recv_sem=rsem.at[number],
            device_id=device, device_id_type=MESH,
        )

    def each(sends, items, act):
        if all(wrapped is None for _, wrapped in items):

            @pl.when(sends)
            def _():
                for copy, _ in items:
                    act(copy)

            return
        inner = [copy for copy, wrapped in items if wrapped is None or not wrapped[1]]
        if inner:

            @pl.when(sends & middle)
            def _():
                for copy in inner:
                    act(copy)

        @pl.when(sends & outer)
        def _():
            for copy, wrapped in items:
                if wrapped is None:
                    act(copy)
                elif wrapped[1]:
                    pl.when(wraps(wrapped[0]))(functools.partial(act, copy))
                else:
                    pl.when(jnp.logical_not(wraps(wrapped[0])))(functools.partial(act, copy))

    def launch(sends, items):
        launched.append((sends, items))
        each(sends, items, lambda copy: copy.start())

    def drain(groups):
        for sends, items in groups:
            each(sends, items, lambda copy: copy.wait_send())

    def landed(ref, number):
        pltpu.make_async_remote_copy(
            src_ref=ref, dst_ref=ref, send_sem=ssem.at[0], recv_sem=rsem.at[number],
            device_id=up, device_id_type=MESH,
        ).wait_recv()

    always = t >= 0

    def slab(ref, side=0):
        return ref.at[pl.ds(2 + 2 * side, 2)]

    def slabs(ref):
        return ref.at[pl.ds(0, 4)]

    def halo(ref, number):
        return [(message(slab(ref), slab(ref, -by), number, at(by)), None) for by in (1, -1)]

    def chunk(ref, k, side=0):
        return ref.at[2 + k // 2 + 2 * side, pl.ds(64 * (k % 2), 64)]

    def crossing(src, dst, number, sides):
        out = [(message(chunk(src, k), chunk(dst, k), number + 2 * k, up), None) for k in range(CHUNKS)]
        return out + [(message(slab(src), slab(dst, -by), sides, at(by, 2)), (by, True)) for by in (1, -1)]

    def forward(ref, k, number):
        return [(message(chunk(ref, k), chunk(ref, k, -by), number, at(by)), (by, False)) for by in (1, -1)]

    def sides(src, dst, number):
        return [(message(slab(src, k), slab(dst, k), number, up), None) for k in (-1, 1)]

    def plane(by, device, wrapped):
        return (message(ic.at[REACH], ic.at[REACH - by], IC, device), wrapped)

    right_guess, left_guess = halo(g, GUESS)
    launch(low & (c == 0), [left_guess])
    for sender, sign in ((even, 1), (odd, -1)):
        offsets = [sign * by for by in range(1, REACH + 1)]
        launch(sender & low, [plane(by, at(by), (by, False)) for by in offsets[:DEEP]])
        launch(
            sender & high,
            [plane(by, at(by), None) for by in offsets]
            + [plane(by, at(by, opposite), (by, True)) for by in offsets[:DEEP]],
        )
    launch(always, [right_guess])
    launch(high | (c > 0), [left_guess])
    launch(even, [(message(slab(g), slab(f), CORE, up), None)])
    launch(t == 0, [(message(slab(i6), slab(f, -by), SIDES, at(by)), (by, False)) for by in (1, -1)])
    launch(t == 2, [(message(slab(i6), slab(f, -by), SIDES, at(by, 0)), (by, True)) for by in (1, -1)])

    def start_planes(reach):
        return [
            (message(v.at[DEEP, 0], v.at[DEEP - sign * by, 0], STARTS, at(sign * by)), None)
            for by in range(1, reach + 1) for sign in (1, -1)
        ]

    @pl.when(odd)
    def _():
        landed(slab(f), CORE)
        v[DEEP, 0] = restricted(f, 2)

    launch(odd, start_planes(2))

    answers = 1 + around
    crossed = crossing(g, f, A_CHUNK, SIDES)

    @pl.when((t == 1) & soon)
    def _():
        pl.semaphore_wait(answer, answers)

    launch((t == 1) & soon, crossed)

    @pl.when(even)
    def _():
        pl.when(low)(lambda: landed(ic.at[pl.ds(REACH - DEEP, DEEP)], IC))
        pl.when(high)(lambda: landed(ic.at[pl.ds(0, REACH)], IC))

    @pl.when(odd)
    def _():
        pl.when(low)(lambda: landed(ic.at[pl.ds(REACH + 1, DEEP)], IC))
        pl.when(high)(lambda: landed(ic.at[pl.ds(REACH + 1, REACH)], IC))

    left, right = ic.at[pl.ds(0, REACH)], ic.at[pl.ds(REACH + 1, REACH)]
    launch(even, [(message(left, left, SWAP, up), None)])
    launch(odd, [(message(right, right, SWAP, down), None)])
    pl.when(even)(lambda: landed(right, SWAP))
    pl.when(odd)(lambda: landed(left, SWAP))

    for j in range(2 * REACH + 1):
        sa[j] = ic[j]

    sb[0] = own
    sb[2 * REACH] = own

    def two_steps(_, carry):
        for j in range(1, 2 * REACH):
            sb[j] = euler(sa[j - 1], sa[j], sa[j + 1])
        for j in range(2, 2 * REACH - 1):
            sa[j] = euler(sb[j - 1], sb[j], sb[j + 1])
        return carry

    lax.fori_loop(0, t, two_steps, 0)
    for j in range(REACH - 2, REACH + 3):
        sb[j] = euler(sa[j - 1], sa[j], sa[j + 1])
    for j in range(3):
        k = REACH - 1 + j
        w[0, j] = sa[k]
        w[1, j] = sb[k]
        w[2, j] = euler(sb[k - 1], sb[k], sb[k + 1])

    landed(slabs(g), GUESS)
    launch(even, sides(g, f, SIDES))

    for k in range(CHUNKS):
        pl.when(t == 2)(lambda k=k: landed(chunk(f, k), A_CHUNK + 2 * k))
        launch(t == 2, forward(f, k, SIDES))

    @pl.when(t == 2)
    def _():
        v[DEEP, 0] = restricted(f, 2)

    @pl.when(t == 0)
    def _():
        for j in range(2 * DEEP + 1):
            v[j, 0] = ic[REACH - DEEP + j]

    launch(t == 2, start_planes(4))
    landed(slabs(f), SIDES)

    old = [restricted(g, 2 * j) for j in range(3)]
    shifts = [[w[m, j] - old[j] for j in range(3)] for m in range(3)]
    fine_sweep((g, g, g), shifts, f, z1, z2, q1, q2, d2, n1, 2, n2, 2)

    first = list(launched)
    v[DEEP, 1] = restricted(n1, 2)
    v[DEEP, 2] = restricted(n2, 2)
    va[...] = mix(A, [v[DEEP, m] for m in range(3)])

    def node_planes(by):
        return (message(v.at[DEEP, pl.ds(1, 2)], v.at[DEEP - by, pl.ds(1, 2)], NODES, at(by)), None)

    def sum_plane(by):
        return (message(va, v.at[DEEP - by, 1], NODES, at(by)), None)

    launch(even, [node_planes(by) for by in near[:8]] + [sum_plane(by) for by in near[8:]])
    launch(odd, [node_planes(by) for by in near[:4]] + [sum_plane(by) for by in near[4:6]])
    launch(even, [(message(slab(n2), slab(f2), CORE2, up), None)])

    @pl.when((t == 1) & later)
    def _():
        pl.semaphore_wait(answer, answers)

    launch((t == 1) & later, crossed)

    n_halo = halo(n2, N2) + halo(n1, N1)
    launch(high & edge, n_halo)
    n_inner = [(copy, (by, False)) for (copy, _), by in zip(n_halo, (1, -1, 1, -1))]
    n_around = [(copy, (by, True)) for (copy, _), by in zip(n_halo, (1, -1, 1, -1))]
    launch(low & edge, n_inner)
    launch((t == 1) & (c == ns - 1), n_around)
    pl.when(t == 2)(lambda: landed(s.at[DEEP], CROSS))
    launch(
        t == 2,
        [(message(s.at[DEEP], s.at[DEEP - by], SPREAD, at(by)), (by, False)) for by in near],
    )
    launch(high & inland, n_halo)
    drain(first)

    @pl.when(even)
    def _():
        pl.when(high)(lambda: landed(v.at[pl.ds(0, 8), 0], STARTS))
        landed(v.at[pl.ds(0, 6)], NODES)

    @pl.when(odd)
    def _():
        landed(v.at[pl.ds(0, 4), 0], STARTS)
        landed(v.at[pl.ds(0, 5), pl.ds(1, 2)], NODES)


    launch((t == 0) & (c == ns - 1), n_around)
    crossed = crossing(n2, f2, B_CHUNK, SIDES2)
    launch((t == 1) & later, crossed)

    for k in range(CHUNKS):
        pl.when(t == 2)(lambda k=k: landed(chunk(f2, k), B_CHUNK + 2 * k))
        launch(t == 2, forward(f2, k, SIDES2))

    def forcing(weights, out, j, sums=()):
        z = [v[k, 1] if k in sums else mix(weights, [v[k, m] for m in range(3)]) for k in (j - 1, j, j + 1)]
        cubes = mix(weights, [cube(v[j, m]) for m in range(3)])
        out[j] = 0.25 * coarse_sum(*z) - 0.5 * z[1] - cubes

    def forcings(reach):
        for j in range(DEEP - reach, DEEP + reach + 1):
            forcing(A, c1, j, (DEEP - reach - 1, DEEP + reach + 1))
            if abs(j - DEEP) < reach:
                forcing(B, c2, j)

    def chain(reach):
        for j in range(DEEP - reach, DEEP + reach + 1):
            t1[j] = euler(s[j - 1], s[j], s[j + 1]) + c1[j]
        for j in range(DEEP - reach + 1, DEEP + reach):
            t2[j] = euler(t1[j - 1], t1[j], t1[j + 1]) + c2[j]

    pl.when(even)(lambda: forcings(4))
    pl.when(odd)(lambda: forcings(2))

    @pl.when(t == 0)
    def _():
        f2[0:2] = f[0:2]
        f2[4:6] = f[4:6]
        for j in range(2 * DEEP + 1):
            s[j] = ic[REACH - DEEP + j]

    pl.when(t == 2)(lambda: landed(s.at[pl.ds(0, 10)], SPREAD))

    pl.when(even)(lambda: chain(4))
    launch(even, [(message(t2.at[pl.ds(2, 7)], s.at[pl.ds(2, 7)], PAIR, up), None)])

    @pl.when(odd)
    def _():
        landed(s.at[pl.ds(2, 7)], PAIR)
        chain(2)

    launch(
        t == 1,
        [(message(t2.at[DEEP], s.at[DEEP], CROSS, up), None)]
        + [(message(t2.at[DEEP], s.at[DEEP - by], SPREAD, at(by, 2)), (by, True)) for by in near],
    )
    launch((t == 1) & soon, crossed)

    launch(low & inland, n_halo)
    launch(low & (c == 0), n_around)

    landed(slabs(n2), N2)
    launch(even, sides(n2, f2, SIDES2))
    landed(slabs(n1), N1)

    pl.when(odd)(lambda: landed(slab(f2), CORE2))
    pl.when(t > 0)(lambda: landed(slabs(f2), SIDES2))

    shifts = []
    for m, level in enumerate((s, t1, t2)):
        shifts.append([level[DEEP - 1 + j] - v[DEEP - 1 + j, m] for j in range(3)])
    fine_sweep((f, n1, n2), shifts, f2, z1, z2, q1, q2, d2, None, 0, out_ref, 0)

    drain(launched[len(first) :])


def interleave(x_ref, out_ref, halves):
    for plane in range(2):
        for row in range(2):
            for col in range(2):
                halves[col, pl.ds(64 * plane + row, 32, stride=2), :] = sub(x_ref, plane, 2 * row + col)
    wide = permuted(jnp.concatenate([halves[0], halves[1]], axis=1), perm_matrix(False))
    out_ref[0, 0] = wide[:64]
    out_ref[0, 1] = wide[64:]


def solution(mesh):
    ns, nt = mesh.shape["space"], mesh.shape["tm"]
    vmem = pl.BlockSpec(memory_space=pltpu.VMEM)

    def local(initial, guess):
        slab6 = pltpu.VMEM((6, 128, 128), jnp.float32)

        def planes(*lead):
            return pltpu.VMEM((*lead, 32, 128), jnp.float32)

        last = pl.pallas_call(
            functools.partial(kernel, ns, nt),
            out_shape=pltpu.VMEM((2, 128, 128), jnp.float32),
            in_specs=[pl.BlockSpec(memory_space=pltpu.HBM)] * 2,
            out_specs=vmem,
            scratch_shapes=[pltpu.VMEM((4, 64, 256), jnp.float32)]
            + [slab6] * 11
            + [planes(2 * REACH + 1)] * 3
            + [planes(3, 3), planes(2 * DEEP + 1, 3), planes()]
            + [planes(2 * DEEP + 1)] * 5
            + [pltpu.VMEM((2, 256, 128), jnp.float32)]
            + [pltpu.SemaphoreType.DMA((160,)), pltpu.SemaphoreType.DMA((24,))]
            + [pltpu.SemaphoreType.DMA((2,)), pltpu.SemaphoreType.REGULAR, pltpu.SemaphoreType.REGULAR],
            compiler_params=pltpu.CompilerParams(
                collective_id=0, has_side_effects=True, vmem_limit_bytes=32 << 20
            ),
            name="pfasst",
        )(*(pltpu.with_memory_space_constraint(x, pltpu.HBM) for x in (initial, guess)))
        return pl.pallas_call(
            interleave,
            out_shape=jax.ShapeDtypeStruct(guess.shape, jnp.float32),
            in_specs=[vmem],
            out_specs=vmem,
            scratch_shapes=[pltpu.VMEM((2, 128, 128), jnp.float32)],
            compiler_params=pltpu.CompilerParams(vmem_limit_bytes=32 << 20),
            name="interleave",
        )(last)

    return jax.shard_map(
        local,
        mesh=mesh,
        in_specs=(P("space", None, None), P("tm", "space", None, None)),
        out_specs=P("tm", "space", None, None),
        check_vma=False,
    )
```

```python
import functools

import jax
import jax.numpy as jnp
from jax import lax
from jax.experimental import pallas as pl
from jax.experimental.pallas import tpu as pltpu
from jax.sharding import PartitionSpec as P

MESH = pl.DeviceIdType.MESH
DT, H = 0.24, 0.12
A = (DT * 5.0 / 24.0 - H, DT / 3.0, -DT / 24.0)
B = (-DT / 24.0, DT / 3.0 - H, DT * 5.0 / 24.0)
REACH = 9
DEEP = 5


def split(x):
    high = x.astype(jnp.bfloat16)
    rest = x - high.astype(jnp.float32)
    mid = rest.astype(jnp.bfloat16)
    low = (rest - mid.astype(jnp.float32)).astype(jnp.bfloat16)
    return jnp.concatenate([high, mid, low], axis=0)


def permuted(x, perm):
    rows = x.shape[0]
    out = jnp.dot(split(x), perm, preferred_element_type=jnp.float32)
    return out[:rows] + (out[rows : 2 * rows] + out[2 * rows :])


def perm_matrix(to_parity):
    i = lax.broadcasted_iota(jnp.int32, (256, 256), 0)
    j = lax.broadcasted_iota(jnp.int32, (256, 256), 1)
    wide, packed = (i, j) if to_parity else (j, i)
    lane = jnp.where(packed < 128, 2 * packed, 2 * packed - 255)
    return jnp.where(wide == lane, 1.0, 0.0).astype(jnp.bfloat16)


def lane_roll(x, by):
    return pltpu.roll(x, by % 128, 1)


def row_roll(x, by):
    return pltpu.roll(x, by % 32, 0)


def coarse_sum(below, x, above):
    total = below + above
    total = total + lane_roll(x, 1) + lane_roll(x, -1)
    return total + row_roll(x, 1) + row_roll(x, -1)


def euler(below, x, above):
    return 0.25 * H * coarse_sum(below, x, above) + x * ((1.0 - 0.5 * H) - H * (x * x))


def cube(x):
    return x * x * x


def mix(weights, values):
    return weights[0] * values[0] + weights[1] * values[1] + weights[2] * values[2]


def sub(ref, plane, part):
    return ref[plane, 32 * part : 32 * part + 32, :]


def restricted(ref, first):
    total = None
    for plane in (first, first + 1):
        for part in range(4):
            piece = sub(ref, plane, part)
            total = piece if total is None else total + piece
    return 0.125 * total


def fine_sum(ref, plane, part):
    row, col = part // 2, part % 2
    beside = sub(ref, plane, row * 2 + 1 - col)
    over = sub(ref, plane, (1 - row) * 2 + col)
    total = sub(ref, plane - 1, part) + sub(ref, plane + 1, part)
    total = total + beside + lane_roll(beside, 1 if col == 0 else -1)
    return total + over + row_roll(over, 1 if row == 0 else -1)


def fine_sweep(nodes, shifts, start, z1, z2, q1, q2, d2, out1, first1, out2, first2):
    for plane in range(6):
        for part in range(4):
            rows = slice(32 * part, 32 * part + 32)
            u = [sub(nodes[m], plane, part) + shifts[m][plane // 2] for m in range(3)]
            n0 = sub(start, plane, part)
            z = H * n0 + mix(A, u)
            z1[plane, rows, :] = z
            if 1 <= plane <= 4:
                cubes = [cube(v) for v in u]
                q1[plane, rows, :] = n0 - 5.0 * z - (H * cube(n0) + mix(A, cubes))
                d2[plane, rows, :] = mix(B, u)
                if 2 <= plane <= 3:
                    q2[plane, rows, :] = mix(B, cubes)
    for plane in range(1, 5):
        for part in range(4):
            rows = slice(32 * part, 32 * part + 32)
            n1 = sub(q1, plane, part) + fine_sum(z1, plane, part)
            z = H * n1 + sub(d2, plane, part)
            z2[plane, rows, :] = z
            if 2 <= plane <= 3:
                if out1 is not None:
                    out1[first1 + plane - 2, rows, :] = n1
                q2[plane, rows, :] = n1 - 5.0 * z - (H * cube(n1) + sub(q2, plane, part))
    for plane in range(2, 4):
        for part in range(4):
            rows = slice(32 * part, 32 * part + 32)
            out2[first2 + plane - 2, rows, :] = sub(q2, plane, part) + fine_sum(z2, plane, part)


IC, SWAP, GUESS, CORE, SIDES, STARTS, NODES, N1, N2, CORE2, SIDES2, CROSS, SPREAD, PAIR, A_CHUNK, B_CHUNK = range(16)
CHUNKS = 4


def kernel(
    ns, nt,
    init_ref, guess_ref, out_ref,
    raw, g, f, n1, n2, f2, i6,
    z1, z2, q1, q2, d2,
    ic, sa, sb, w, v, va, c1, c2, s, t1, t2, halves,
    ssem, rsem, lsem, answer, passed,
):
    t = lax.axis_index("tm")
    c = lax.axis_index("space")
    even = lax.rem(t, 2) == 0
    odd = lax.rem(t, 2) == 1
    low, high = t < 2, t >= 2
    opposite = lax.rem(t + 2, nt)
    middle = (c >= REACH) & (c < ns - REACH)
    outer = (c < REACH) | (c >= ns - REACH)
    edge = (c < DEEP) | (c >= ns - DEEP)
    soon = (c < DEEP) | (c >= 3 * ns // 4)
    later = (c >= DEEP) & (c < 3 * ns // 4)
    inland = (c >= DEEP) & (c < ns - DEEP)

    loads = [
        pltpu.make_async_copy(guess_ref.at[0], raw.at[pl.ds(0, 2)], lsem.at[0]),
        pltpu.make_async_copy(init_ref, raw.at[pl.ds(2, 2)], lsem.at[1]),
    ]
    for load in loads:
        load.start()

    def wraps(by):
        return (c + by >= ns) if by > 0 else (c + by < 0)

    def at(by, row=None):
        return (t if row is None else row, lax.rem(c + by + ns, ns))

    up = (jnp.minimum(t + 1, nt - 1), c)
    down = (jnp.maximum(t - 1, 0), c)

    barrier = pltpu.get_barrier_semaphore()
    row = jnp.minimum(t, 2)

    def signal(semaphore, device):
        pl.semaphore_signal(semaphore, inc=1, device_id=device, device_id_type=MESH)

    near = [sign * by for by in range(1, DEEP + 1) for sign in (1, -1)]

    @pl.when(edge)
    def _():
        for by in near:

            @pl.when(wraps(by))
            def _(by=by):
                signal(barrier, at(by, row))
                pl.when(low)(lambda: signal(barrier, at(by, 2)))
                pl.when(t == 1)(lambda: signal(barrier, at(by, 3)))

    pl.when(even)(lambda: signal(barrier, up))
    pl.when(odd)(lambda: signal(barrier, down))
    pl.when(t == 1)(lambda: signal(barrier, (3, c)))
    for by in near:
        pl.when(jnp.logical_not(wraps(by)))(lambda by=by: signal(barrier, at(by, row)))

    @pl.when(high & even)
    def _():
        for by in range(DEEP + 1, REACH + 1):
            signal(barrier, at(-by))

    @pl.when(high & odd)
    def _():
        for by in range(DEEP + 1, REACH + 1):
            signal(barrier, at(by, 2))

    around = 0
    for by in near:
        around = around + jnp.where(wraps(by), 1, 0)
    count = len(near)
    expected = jnp.where(low, count + 1, jnp.where(t == 2, 2 * count + 2 * (REACH - DEEP) + 1 + 2 * around, 2 + around))

    for load in loads:
        load.wait()
    packed = permuted(jnp.concatenate([raw[k] for k in range(4)], axis=0), perm_matrix(True))
    halves[0] = packed[:, :128]
    halves[1] = packed[:, 128:]
    for plane in range(2):
        for row in range(2):
            for col in range(2):
                part = slice(64 * row + 32 * col, 64 * row + 32 * col + 32)
                g[2 + plane, part, :] = halves[col, pl.ds(64 * plane + row, 32, stride=2), :]
                i6[2 + plane, part, :] = halves[col, pl.ds(128 + 64 * plane + row, 32, stride=2), :]
    own = restricted(i6, 2)
    ic[REACH] = own

    @pl.when(t == 0)
    def _():
        f[2:4] = i6[2:4]
        f2[2:4] = i6[2:4]
        for j in range(REACH - DEEP):
            ic[j] = own

    @pl.when(t == 1)
    def _():
        for j in range(REACH + DEEP + 1, 2 * REACH + 1):
            ic[j] = own

    pl.semaphore_wait(barrier, expected)

    @pl.when(t == 3)
    def _():
        signal(answer, (1, c))

        @pl.when(edge)
        def _():
            for by in near:
                pl.when(wraps(by))(lambda by=by: signal(answer, at(by, 1)))

        pl.semaphore_wait(passed, 1)

    @pl.when(t == 2)
    def _():
        signal(passed, up)

    ids = iter(range(200))
    launched = []

    def message(src, dst, number, device):
        return pltpu.make_async_remote_copy(
            src_ref=src, dst_ref=dst, send_sem=ssem.at[next(ids)], recv_sem=rsem.at[number],
            device_id=device, device_id_type=MESH,
        )

    def each(sends, items, act):
        if all(wrapped is None for _, wrapped in items):

            @pl.when(sends)
            def _():
                for copy, _ in items:
                    act(copy)

            return
        inner = [copy for copy, wrapped in items if wrapped is None or not wrapped[1]]
        if inner:

            @pl.when(sends & middle)
            def _():
                for copy in inner:
                    act(copy)

        @pl.when(sends & outer)
        def _():
            for copy, wrapped in items:
                if wrapped is None:
                    act(copy)
                elif wrapped[1]:
                    pl.when(wraps(wrapped[0]))(functools.partial(act, copy))
                else:
                    pl.when(jnp.logical_not(wraps(wrapped[0])))(functools.partial(act, copy))

    def launch(sends, items):
        launched.append((sends, items))
        each(sends, items, lambda copy: copy.start())

    def drain(groups):
        for sends, items in groups:
            each(sends, items, lambda copy: copy.wait_send())

    def landed(ref, number):
        pltpu.make_async_remote_copy(
            src_ref=ref, dst_ref=ref, send_sem=ssem.at[0], recv_sem=rsem.at[number],
            device_id=up, device_id_type=MESH,
        ).wait_recv()

    always = t >= 0

    def slab(ref, side=0):
        return ref.at[pl.ds(2 + 2 * side, 2)]

    def slabs(ref):
        return ref.at[pl.ds(0, 4)]

    def halo(ref, number):
        return [(message(slab(ref), slab(ref, -by), number, at(by)), None) for by in (1, -1)]

    def chunk(ref, k, side=0):
        return ref.at[2 + k // 2 + 2 * side, pl.ds(64 * (k % 2), 64)]

    def crossing(src, dst, number, sides):
        out = [(message(chunk(src, k), chunk(dst, k), number + 2 * k, up), None) for k in range(CHUNKS)]
        return out + [(message(slab(src), slab(dst, -by), sides, at(by, 2)), (by, True)) for by in (1, -1)]

    def forward(ref, k, number):
        return [(message(chunk(ref, k), chunk(ref, k, -by), number, at(by)), (by, False)) for by in (1, -1)]

    def sides(src, dst, number):
        return [(message(slab(src, k), slab(dst, k), number, up), None) for k in (-1, 1)]

    def plane(by, device, wrapped):
        return (message(ic.at[REACH], ic.at[REACH - by], IC, device), wrapped)

    right_guess, left_guess = halo(g, GUESS)
    launch(low & (c == 0), [left_guess])
    for sender, sign in ((even, 1), (odd, -1)):
        offsets = [sign * by for by in range(1, REACH + 1)]
        launch(sender & low, [plane(by, at(by), (by, False)) for by in offsets[:DEEP]])
        launch(
            sender & high,
            [plane(by, at(by), None) for by in offsets]
            + [plane(by, at(by, opposite), (by, True)) for by in offsets[:DEEP]],
        )
    launch(always, [right_guess])
    launch(high | (c > 0), [left_guess])
    launch(even, [(message(slab(g), slab(f), CORE, up), None)])
    launch(t == 0, [(message(slab(i6), slab(f, -by), SIDES, at(by)), (by, False)) for by in (1, -1)])
    launch(t == 2, [(message(slab(i6), slab(f, -by), SIDES, at(by, 0)), (by, True)) for by in (1, -1)])

    def start_planes(reach):
        return [
            (message(v.at[DEEP, 0], v.at[DEEP - sign * by, 0], STARTS, at(sign * by)), None)
            for by in range(1, reach + 1) for sign in (1, -1)
        ]

    @pl.when(odd)
    def _():
        landed(slab(f), CORE)
        v[DEEP, 0] = restricted(f, 2)

    launch(odd, start_planes(2))

    answers = 1 + around
    crossed = crossing(g, f, A_CHUNK, SIDES)

    @pl.when((t == 1) & soon)
    def _():
        pl.semaphore_wait(answer, answers)

    launch((t == 1) & soon, crossed)

    @pl.when(even)
    def _():
        pl.when(low)(lambda: landed(ic.at[pl.ds(REACH - DEEP, DEEP)], IC))
        pl.when(high)(lambda: landed(ic.at[pl.ds(0, REACH)], IC))

    @pl.when(odd)
    def _():
        pl.when(low)(lambda: landed(ic.at[pl.ds(REACH + 1, DEEP)], IC))
        pl.when(high)(lambda: landed(ic.at[pl.ds(REACH + 1, REACH)], IC))

    left, right = ic.at[pl.ds(0, REACH)], ic.at[pl.ds(REACH + 1, REACH)]
    launch(even, [(message(left, left, SWAP, up), None)])
    launch(odd, [(message(right, right, SWAP, down), None)])
    pl.when(even)(lambda: landed(right, SWAP))
    pl.when(odd)(lambda: landed(left, SWAP))

    for j in range(2 * REACH + 1):
        sa[j] = ic[j]

    sb[0] = own
    sb[2 * REACH] = own

    def two_steps(_, carry):
        for j in range(1, 2 * REACH):
            sb[j] = euler(sa[j - 1], sa[j], sa[j + 1])
        for j in range(2, 2 * REACH - 1):
            sa[j] = euler(sb[j - 1], sb[j], sb[j + 1])
        return carry

    lax.fori_loop(0, t, two_steps, 0)
    for j in range(REACH - 2, REACH + 3):
        sb[j] = euler(sa[j - 1], sa[j], sa[j + 1])
    for j in range(3):
        k = REACH - 1 + j
        w[0, j] = sa[k]
        w[1, j] = sb[k]
        w[2, j] = euler(sb[k - 1], sb[k], sb[k + 1])

    landed(slabs(g), GUESS)
    launch(even, sides(g, f, SIDES))

    for k in range(CHUNKS):
        pl.when(t == 2)(lambda k=k: landed(chunk(f, k), A_CHUNK + 2 * k))
        launch(t == 2, forward(f, k, SIDES))

    @pl.when(t == 2)
    def _():
        v[DEEP, 0] = restricted(f, 2)

    @pl.when(t == 0)
    def _():
        for j in range(2 * DEEP + 1):
            v[j, 0] = ic[REACH - DEEP + j]

    launch(t == 2, start_planes(4))
    landed(slabs(f), SIDES)

    old = [restricted(g, 2 * j) for j in range(3)]
    shifts = [[w[m, j] - old[j] for j in range(3)] for m in range(3)]
    fine_sweep((g, g, g), shifts, f, z1, z2, q1, q2, d2, n1, 2, n2, 2)

    first = list(launched)
    v[DEEP, 1] = restricted(n1, 2)
    v[DEEP, 2] = restricted(n2, 2)
    va[...] = mix(A, [v[DEEP, m] for m in range(3)])

    def node_planes(by):
        return (message(v.at[DEEP, pl.ds(1, 2)], v.at[DEEP - by, pl.ds(1, 2)], NODES, at(by)), None)

    def sum_plane(by):
        return (message(va, v.at[DEEP - by, 1], NODES, at(by)), None)

    launch(even, [node_planes(by) for by in near[:8]] + [sum_plane(by) for by in near[8:]])
    launch(odd, [node_planes(by) for by in near[:4]] + [sum_plane(by) for by in near[4:6]])
    launch(even, [(message(slab(n2), slab(f2), CORE2, up), None)])

    @pl.when((t == 1) & later)
    def _():
        pl.semaphore_wait(answer, answers)

    launch((t == 1) & later, crossed)

    n_halo = halo(n2, N2) + halo(n1, N1)
    launch(high, n_halo)
    n_inner = [(copy, (by, False)) for (copy, _), by in zip(n_halo, (1, -1, 1, -1))]
    n_around = [(copy, (by, True)) for (copy, _), by in zip(n_halo, (1, -1, 1, -1))]
    launch(low & edge, n_inner)
    launch((t == 1) & (c == ns - 1), n_around)
    pl.when(t == 2)(lambda: landed(s.at[DEEP], CROSS))
    launch(
        t == 2,
        [(message(s.at[DEEP], s.at[DEEP - by], SPREAD, at(by)), (by, False)) for by in near],
    )
    drain(first)

    @pl.when(even)
    def _():
        pl.when(high)(lambda: landed(v.at[pl.ds(0, 8), 0], STARTS))
        landed(v.at[pl.ds(0, 6)], NODES)

    @pl.when(odd)
    def _():
        landed(v.at[pl.ds(0, 4), 0], STARTS)
        landed(v.at[pl.ds(0, 5), pl.ds(1, 2)], NODES)


    launch((t == 0) & (c == ns - 1), n_around)
    crossed = crossing(n2, f2, B_CHUNK, SIDES2)
    launch((t == 1) & later, crossed)

    for k in range(CHUNKS):
        pl.when(t == 2)(lambda k=k: landed(chunk(f2, k), B_CHUNK + 2 * k))
        launch(t == 2, forward(f2, k, SIDES2))

    def forcing(weights, out, j, sums=()):
        z = [v[k, 1] if k in sums else mix(weights, [v[k, m] for m in range(3)]) for k in (j - 1, j, j + 1)]
        cubes = mix(weights, [cube(v[j, m]) for m in range(3)])
        out[j] = 0.25 * coarse_sum(*z) - 0.5 * z[1] - cubes

    def forcings(reach):
        for j in range(DEEP - reach, DEEP + reach + 1):
            forcing(A, c1, j, (DEEP - reach - 1, DEEP + reach + 1))
            if abs(j - DEEP) < reach:
                forcing(B, c2, j)

    def chain(reach):
        for j in range(DEEP - reach, DEEP + reach + 1):
            t1[j] = euler(s[j - 1], s[j], s[j + 1]) + c1[j]
        for j in range(DEEP - reach + 1, DEEP + reach):
            t2[j] = euler(t1[j - 1], t1[j], t1[j + 1]) + c2[j]

    pl.when(even)(lambda: forcings(4))
    pl.when(odd)(lambda: forcings(2))

    @pl.when(t == 0)
    def _():
        f2[0:2] = f[0:2]
        f2[4:6] = f[4:6]
        for j in range(2 * DEEP + 1):
            s[j] = ic[REACH - DEEP + j]

    pl.when(t == 2)(lambda: landed(s.at[pl.ds(0, 10)], SPREAD))

    pl.when(even)(lambda: chain(4))
    launch(even, [(message(t2.at[pl.ds(2, 7)], s.at[pl.ds(2, 7)], PAIR, up), None)])

    @pl.when(odd)
    def _():
        landed(s.at[pl.ds(2, 7)], PAIR)
        chain(2)

    launch(
        t == 1,
        [(message(t2.at[DEEP], s.at[DEEP], CROSS, up), None)]
        + [(message(t2.at[DEEP], s.at[DEEP - by], SPREAD, at(by, 2)), (by, True)) for by in near],
    )
    launch((t == 1) & soon, crossed)

    launch(low & inland, n_halo)
    launch(low & (c == 0), n_around)

    landed(slabs(n2), N2)
    launch(even, sides(n2, f2, SIDES2))
    landed(slabs(n1), N1)

    pl.when(odd)(lambda: landed(slab(f2), CORE2))
    pl.when(t > 0)(lambda: landed(slabs(f2), SIDES2))

    shifts = []
    for m, level in enumerate((s, t1, t2)):
        shifts.append([level[DEEP - 1 + j] - v[DEEP - 1 + j, m] for j in range(3)])
    fine_sweep((f, n1, n2), shifts, f2, z1, z2, q1, q2, d2, None, 0, out_ref, 0)

    drain(launched[len(first) :])


def interleave(x_ref, out_ref, halves):
    for plane in range(2):
        for row in range(2):
            for col in range(2):
                halves[col, pl.ds(64 * plane + row, 32, stride=2), :] = sub(x_ref, plane, 2 * row + col)
    wide = permuted(jnp.concatenate([halves[0], halves[1]], axis=1), perm_matrix(False))
    out_ref[0, 0] = wide[:64]
    out_ref[0, 1] = wide[64:]


def solution(mesh):
    ns, nt = mesh.shape["space"], mesh.shape["tm"]
    vmem = pl.BlockSpec(memory_space=pltpu.VMEM)

    def local(initial, guess):
        slab6 = pltpu.VMEM((6, 128, 128), jnp.float32)

        def planes(*lead):
            return pltpu.VMEM((*lead, 32, 128), jnp.float32)

        last = pl.pallas_call(
            functools.partial(kernel, ns, nt),
            out_shape=pltpu.VMEM((2, 128, 128), jnp.float32),
            in_specs=[pl.BlockSpec(memory_space=pltpu.HBM)] * 2,
            out_specs=vmem,
            scratch_shapes=[pltpu.VMEM((4, 64, 256), jnp.float32)]
            + [slab6] * 11
            + [planes(2 * REACH + 1)] * 3
            + [planes(3, 3), planes(2 * DEEP + 1, 3), planes()]
            + [planes(2 * DEEP + 1)] * 5
            + [pltpu.VMEM((2, 256, 128), jnp.float32)]
            + [pltpu.SemaphoreType.DMA((160,)), pltpu.SemaphoreType.DMA((24,))]
            + [pltpu.SemaphoreType.DMA((2,)), pltpu.SemaphoreType.REGULAR, pltpu.SemaphoreType.REGULAR],
            compiler_params=pltpu.CompilerParams(
                collective_id=0, has_side_effects=True, vmem_limit_bytes=32 << 20
            ),
            name="pfasst",
        )(*(pltpu.with_memory_space_constraint(x, pltpu.HBM) for x in (initial, guess)))
        return pl.pallas_call(
            interleave,
            out_shape=jax.ShapeDtypeStruct(guess.shape, jnp.float32),
            in_specs=[vmem],
            out_specs=vmem,
            scratch_shapes=[pltpu.VMEM((2, 128, 128), jnp.float32)],
            compiler_params=pltpu.CompilerParams(vmem_limit_bytes=32 << 20),
            name="interleave",
        )(last)

    return jax.shard_map(
        local,
        mesh=mesh,
        in_specs=(P("space", None, None), P("tm", "space", None, None)),
        out_specs=P("tm", "space", None, None),
        check_vma=False,
    )
```
